128 devices in a mesh: dp: 16 (over y, x), mp: 8 (over z, core).
Axes of the slice: x: 4, y: 4, z: 4, core: 2. Of those that a mesh axis runs over, the one named last changes fastest.
Arguments:
- inner_before_nonlinear: bfloat16 [8192, 10240], P('dp', 'mp'), may hold values from -6 to 6
- layer_exit_derivative: bfloat16 [8192, 5120], P('dp', 'mp'), may hold values from -6 to 6
- contract_weights: bfloat16 [10240, 5120], P('mp'), may hold values from -0.0625 to 0.0625
- copy_tile_indicator: int32 [16, 8, 51200], P('dp', 'mp'), may hold values from 0 to 1, as said below
- span_opening_tile: int32 [17], replicated, may hold values from 0 to 51200, as said below
- remaining_tile_flags: int32 [8, 51200], P('mp'), may hold values from 0 to 1, as said below
Outputs:
- pre_grad: bfloat16 [8192, 10240], P('dp', 'mp')
- grad_blocks: float32 [8, 6400, 128], P('mp')
The draws below stay inside these ranges and needn't reach their ends.
Inputs may be any that keep to these rules, and one draw needn't show every extreme that they name: `copy_tile_indicator`: in every region, at most 1600 ones of one replica and one index of mp; in every draw one region holds exactly 1600 from every replica. `span_opening_tile`: starts at 0 and ends at 51200; each region holds 1600 to 4800 blocks, and some region exactly 4800. `remaining_tile_flags`: at most 400 ones in each region of each row; some region holds exactly 400.
All inputs are finite; a program needn't handle non-finite values.
Results may differ from the reference program's by a relative error of at most 0.013.
Values may be sent and summed in bfloat16 or wider, within the bound.
A program may use at most 192 MiB of HBM per device.

```python
import math
import jax
import jax.numpy as jnp
from jax import lax

D = 5120
FF = 10240
TOK = 512
NBLK = 51200
BASE = 3200
CAPS = 1600
PEAK_SAVED_TILES = 400
TOKENS = 8192
N_DP = 16
N_MP = 8


def region_bounds(key):
    pair_key, pick_key, order_key = jax.random.split(jax.random.fold_in(key, 11), 3)
    half_count = N_DP // 2
    spread = jax.random.randint(pair_key, (half_count,), 0, BASE // 2 + 1)
    forced = jax.random.randint(pick_key, (), 0, half_count)
    spread = jnp.where(jnp.arange(half_count) == forced, BASE // 2, spread)
    widths = jnp.stack([BASE + spread, BASE - spread], axis=1).reshape(N_DP)
    widths = widths[jax.random.permutation(order_key, N_DP)]
    return jnp.concatenate([jnp.zeros((1,), jnp.int32), jnp.cumsum(widths).astype(jnp.int32)])


def region_index(bounds):
    return jnp.sum(jnp.arange(NBLK)[:, None] >= bounds[None, 1:N_DP], axis=1).astype(jnp.int32)


def within_rank(chosen, bounds, region_of):
    cumulative_tally = jnp.cumsum(chosen, axis=-1).astype(jnp.int32)
    padded = jnp.concatenate([jnp.zeros(cumulative_tally.shape[:-1] + (1,), jnp.int32), cumulative_tally], axis=-1)
    return cumulative_tally - jnp.take(padded, bounds[region_of], axis=-1)


def draw_span_opening_tile(key, part):
    return region_bounds(key)


def draw_copy_tile_indicator(key, part):
    bounds = region_bounds(key)
    region_of = region_index(bounds)
    key = jax.random.fold_in(key, 3)
    level_key, coin_key, pick_key = jax.random.split(key, 3)
    levels = jax.random.randint(level_key, (N_DP, 1, 1), 1, 6)
    coins = jax.random.randint(coin_key, (N_DP, N_MP, NBLK), 0, 10)
    chosen = (coins < levels).astype(jnp.int32)
    forced = jax.random.randint(pick_key, (), 0, N_DP)
    chosen = jnp.where((region_of == forced)[None, None, :], 1, chosen).astype(jnp.int32)
    tile_place = within_rank(chosen, bounds, region_of)
    return jnp.where(tile_place <= CAPS, chosen, 0).astype(jnp.int32)


def draw_remaining_tile_flags(key, part):
    bounds = region_bounds(key)
    region_of = region_index(bounds)
    key = jax.random.fold_in(key, 5)
    coin_key, pick_key = jax.random.split(key, 2)
    coins = jax.random.randint(coin_key, (N_MP, NBLK), 0, 12)
    chosen = (coins == 0).astype(jnp.int32)
    forced = jax.random.randint(pick_key, (), 0, N_DP)
    leading = (region_of == forced) & (jnp.arange(NBLK) - bounds[region_of] < PEAK_SAVED_TILES)
    chosen = jnp.where(leading[None, :], 1, chosen).astype(jnp.int32)
    tile_place = within_rank(chosen, bounds, region_of)
    return jnp.where(tile_place <= PEAK_SAVED_TILES, chosen, 0).astype(jnp.int32)


def block_levels(key, dims, pieces, low, top_value):
    loudness, own = 1.0, jax.random.fold_in(key, 6)
    for axis_at, blocks in pieces:
        steps = jnp.exp(jax.random.uniform(jax.random.fold_in(own, axis_at), (blocks,), jnp.float32, low / len(pieces), top_value / len(pieces)))
        loudness = loudness * jnp.repeat(steps, dims[axis_at] // blocks).reshape([-1 if axis == axis_at else 1 for axis in range(len(dims))])
    return loudness


def gaussian(rng, dims, width, bound, cuts=(), kind=jnp.bfloat16):
    gain = block_levels(rng, dims, cuts, -0.22, 0.18) if cuts else 1.0
    values = jax.random.normal(rng, dims, jnp.float32) * width * gain
    return jnp.minimum(jnp.maximum(values, -bound), bound).astype(kind)


def setup_inputs(seed: int = 0) -> dict:
    streams_of = jax.random.split(jax.random.key(seed), 7)
    return {
        "inner_before_nonlinear": gaussian(streams_of[0], (TOKENS, FF), 1.0, 6.0, ((0, 16), (1, 8))),
        "layer_exit_derivative": gaussian(streams_of[1], (TOKENS, D), 1.0, 6.0, ((0, 16), (1, 8))),
        "contract_weights": gaussian(streams_of[2], (FF, D), FF ** -0.5, 0.0625, ((0, 8),)),
        "copy_tile_indicator": draw_copy_tile_indicator(jax.random.fold_in(streams_of[6], 71), 0),
        "span_opening_tile": draw_span_opening_tile(jax.random.fold_in(streams_of[6], 71), 0),
        "remaining_tile_flags": draw_remaining_tile_flags(jax.random.fold_in(streams_of[6], 71), 0),
    }


half_root = 0.7071067811865476
inv_root_tau = 0.3989422804014327

def gelu_parts(inner_before_nonlinear):
    values = inner_before_nonlinear.astype(jnp.float32)
    normal_cdf = 0.5 * (1.0 + jax.scipy.special.erf(values * half_root))
    density = jnp.exp(-0.5 * values * values) * inv_root_tau
    return (values * normal_cdf, normal_cdf + values * density)

def reference(inner_before_nonlinear, layer_exit_derivative, contract_weights, copy_tile_indicator, span_opening_tile, remaining_tile_flags):
    activation, gelu_slope = gelu_parts(inner_before_nonlinear)
    activation = activation.astype(jnp.bfloat16)
    act_grad = lax.dot_general(layer_exit_derivative, contract_weights, (((1,), (1,)), ((), ())), preferred_element_type=jnp.float32)
    pre_grad = (act_grad * gelu_slope).astype(jnp.bfloat16)
    grad_scale = 1.0 / math.sqrt(TOKENS)

    def add_replica(replica, total):
        first_row = (replica * TOK).astype(jnp.int32)
        rows_act = lax.dynamic_slice_in_dim(activation, first_row, TOK, 0)
        rows_grad = lax.dynamic_slice_in_dim(layer_exit_derivative, first_row, TOK, 0)
        weight_grad = (lax.dot_general(rows_act, rows_grad, (((0,), (0,)), ((), ())), preferred_element_type=jnp.float32) * grad_scale).astype(jnp.bfloat16)
        grad_rows = weight_grad.reshape(N_MP, NBLK, 128).astype(jnp.float32)
        chosen = lax.dynamic_index_in_dim(copy_tile_indicator, replica.astype(jnp.int32), 0, keepdims=False).astype(jnp.float32)
        return total + grad_rows * chosen[:, :, None]
    summed = lax.fori_loop(0, N_DP, add_replica, jnp.zeros((N_MP, NBLK, 128), jnp.float32))
    block_ids = jnp.arange(NBLK, dtype=jnp.int32)
    region_of = lax.optimization_barrier(jnp.sum(block_ids[:, None] >= span_opening_tile[None, 1:N_DP], axis=1)).astype(jnp.int32)
    cumulative_tally = jnp.cumsum(remaining_tile_flags, axis=1).astype(jnp.int32)
    padded = jnp.concatenate([jnp.zeros((N_MP, 1), jnp.int32), cumulative_tally], axis=1)
    tile_place = cumulative_tally - padded[:, span_opening_tile[region_of]]
    retained_tiles = (remaining_tile_flags == 1) & (tile_place <= PEAK_SAVED_TILES)
    slot_index = jnp.where(retained_tiles, region_of[None, :] * PEAK_SAVED_TILES + tile_place - 1, N_DP * PEAK_SAVED_TILES).astype(jnp.int32)
    rows_index = jnp.arange(N_MP, dtype=jnp.int32)[:, None]
    result = jnp.zeros((N_MP, N_DP * PEAK_SAVED_TILES + 1, 128), jnp.float32).at[rows_index, slot_index].set(summed)
    return (pre_grad, result[:, :N_DP * PEAK_SAVED_TILES])
```

```python
import functools
import math

import jax
import jax.numpy as jnp
from jax import lax
from jax.experimental import pallas as pl
from jax.experimental.pallas import tpu as pltpu
from jax.sharding import PartitionSpec as P

half_root = 0.7071067811865476
inv_root_tau = 0.3989422804014327
MESH = pl.DeviceIdType.MESH

TOK = 512
HID = 1280
WIDTH = 5120
PART = 640
PAIR = 2 * PART
LANES = 128
COLS = WIDTH // LANES
NBLK = HID * COLS
KEEP = 400
HALF = TOK // 2
GROUP = 16
SPLIT = ((0, 112, 96), (208, 96, 96))


def slot_sources(flags, copied, starts):
    rows = NBLK // LANES
    flag_rows = flags.reshape(rows, LANES)
    lane = lax.broadcasted_iota(jnp.int32, (LANES, LANES), 0)
    tri = (lane <= lane.T).astype(jnp.bfloat16)
    within = jnp.dot(flag_rows.astype(jnp.bfloat16), tri, preferred_element_type=jnp.float32)
    totals = within[:, LANES - 1]
    before = jnp.sum(
        jnp.where(jnp.arange(rows)[None, :] < jnp.arange(rows)[:, None], totals[None, :], 0.0), axis=1
    )
    upto = (before + totals).astype(jnp.int32)
    totals = totals.astype(jnp.int32)
    block = jnp.arange(NBLK, dtype=jnp.int32)
    base = jnp.sum(jnp.where(block[None, :] < starts[:, None], flags[None, :], 0), axis=1)
    slot = jnp.arange(KEEP, dtype=jnp.int32)
    target = (base[:-1, None] + slot[None, :]).reshape(-1)
    filled = (slot[None, :] < (base[1:] - base[:-1])[:, None]).reshape(-1)
    passed = upto[None, :] <= target[:, None]
    row = jnp.sum(passed.astype(jnp.int32), axis=1)
    rest = target - jnp.sum(jnp.where(passed, totals[None, :], 0), axis=1)
    pick = (row[:, None] == jnp.arange(rows)[None, :]).astype(jnp.bfloat16)
    table = jnp.concatenate(
        [within.astype(jnp.bfloat16), copied.reshape(rows, LANES).astype(jnp.bfloat16)], axis=1
    )
    picked = jnp.dot(pick, table, preferred_element_type=jnp.float32)
    at = jnp.sum((picked[:, :LANES] <= rest[:, None].astype(jnp.float32)).astype(jnp.int32), axis=1)
    kept = jnp.sum(
        jnp.where(jnp.arange(LANES)[None, :] == at[:, None], picked[:, LANES:], 0.0), axis=1
    )
    source = row * LANES + at
    source = (source % COLS) * HID + source // COLS
    return jnp.where(filled & (kept > 0.5), source, NBLK)


def kernel(
    u_ref, g_ref, w_ref, src_ref,
    pre_ref, out_ref,
    wg, wbuf, grad, act_t, slope, acc, send, stage,
    f1a, l1a, r1a, f1b, l1b, r1b, f2a, l2a, r2a, f2b, l2b, r2b,
    local_sem, w_sem, z_send, z_recv, s_send, s_recv, d_send, d_recv,
):
    dp = lax.axis_index("dp")
    mp = lax.axis_index("mp")
    y, x = dp // 4, lax.rem(dp, 4)
    z, core = mp // 2, lax.rem(mp, 2)

    def step(p, d):
        return lax.rem(p + d + 4, 4)

    z_right, z_left, z_far = step(z, 1), step(z, -1), step(z, 2)
    dev_z = ((dp, z_right * 2 + core), (dp, z_left * 2 + core))
    dev_sib = (dp, z * 2 + 1 - core)
    dev_x = ((y * 4 + step(x, 1), mp), (y * 4 + step(x, -1), mp))
    dev_y = ((step(y, 1) * 4 + x, mp), (step(y, -1) * 4 + x, mp))

    barrier = pltpu.get_barrier_semaphore()
    peers = (*dev_z, dev_sib, *dev_x, *dev_y)
    for peer in peers:
        pl.semaphore_signal(barrier, inc=1, device_id=peer, device_id_type=MESH)

    def w_load(zp, slot, sem):
        cols = pl.ds(pl.multiple_of(zp * PAIR, LANES), PAIR)
        return pltpu.make_async_copy(w_ref.at[:, cols], wbuf.at[slot], w_sem.at[sem])

    mine = pl.ds(pl.multiple_of(core * PART, LANES), PART)
    other = pl.ds(pl.multiple_of((1 - core) * PART, LANES), PART)
    own_copy = pltpu.make_async_copy(g_ref, grad.at[z, :, mine], local_sem.at[0])
    own_copy.start()
    loads = [w_load(z, 0, 0), w_load(z_left, 1, 1), w_load(z_right, 2, 2), w_load(z_far, 0, 3)]
    for load in loads[:3]:
        load.start()

    pl.semaphore_wait(barrier, len(peers))

    h0, h1 = pl.ds(0, HALF), pl.ds(HALF, HALF)

    def remote(src, dst, s_sem, r_sem, device):
        return pltpu.make_async_remote_copy(
            src_ref=src, dst_ref=dst, send_sem=s_sem, recv_sem=r_sem, device_id=device, device_id_type=MESH
        )

    def z_copy(n, src, zp, rows, way):
        return remote(src, grad.at[zp, rows, mine], z_send.at[n], z_recv.at[n], dev_z[way])

    def s_copy(n, zp, rows):
        part = grad.at[zp, rows, mine]
        return remote(part, part, s_send.at[n], s_recv.at[n], dev_sib)

    z_own = [
        z_copy(0, g_ref.at[h0], z, h0, 0),
        z_copy(1, g_ref.at[h1], z, h1, 1),
        z_copy(2, g_ref.at[h1], z, h1, 0),
        z_copy(3, g_ref.at[h0], z, h0, 1),
    ]
    s_own = remote(g_ref, grad.at[z, :, mine], s_send.at[0], s_recv.at[0], dev_sib)
    for copy in z_own:
        copy.start()
    s_own.start()
    z_fwd = [
        z_copy(4, grad.at[z_left, h0, mine], z_left, h0, 0),
        z_copy(5, grad.at[z_right, h1, mine], z_right, h1, 1),
    ]
    s_fwd = [
        s_copy(1, z_left, h0),
        s_copy(2, z_right, h1),
        s_copy(3, z_left, h1),
        s_copy(4, z_right, h0),
        s_copy(5, z_far, h0),
        s_copy(6, z_far, h1),
    ]

    wg[pl.ds(NBLK, GROUP), :] = jnp.zeros((GROUP, LANES), jnp.float32)

    def gelu(n, carry):
        tok = pl.ds(pl.multiple_of(lax.rem(n, 4) * LANES, LANES), LANES)
        hid = pl.ds(pl.multiple_of((n // 4) * LANES, LANES), LANES)
        values = u_ref[tok, hid].astype(jnp.float32)
        cdf = 0.5 * (1.0 + lax.erf(values * half_root))
        density = jnp.exp(-0.5 * values * values) * inv_root_tau
        act_t[hid, tok] = (values * cdf).T.astype(jnp.bfloat16)
        slope[tok, hid] = cdf + values * density
        return carry

    lax.fori_loop(0, 4 * (HID // LANES), gelu, 0)

    def weight_grad(zp, n, part_cols, width):
        cols = pl.ds(pl.multiple_of(part_cols + n * width, LANES), width)
        first = zp * (PAIR // LANES) + (part_cols + n * width) // LANES
        for half in range(2):
            product = jnp.dot(
                act_t[pl.ds(half * PART, PART), :], grad[zp, :, cols], preferred_element_type=jnp.float32
            )
            for c in range(width // LANES):
                row = pl.multiple_of((first + c) * HID + half * PART, LANES)
                wg[pl.ds(row, PART), :] = product[:, c * LANES : (c + 1) * LANES]

    def weight_grad_pair(zp):
        def body(n, carry):
            weight_grad(zp, n, 0, 256)
            return carry

        lax.fori_loop(0, PAIR // 256, body, 0)

    def weight_grad_part(zp, which):
        def body(n, carry):
            weight_grad(zp, n, which * PART, LANES)
            return carry

        lax.fori_loop(0, PART // LANES, body, 0)

    def pre_product(zp, slot, rows, mode):
        def body(n, carry):
            hid = pl.ds(pl.multiple_of(n * 256, LANES), 256)
            product = lax.dot_general(
                grad[zp, rows, :], wbuf[slot, hid, :], (((1,), (1,)), ((), ())),
                preferred_element_type=jnp.float32,
            )
            if mode == "first":
                acc[rows, hid] = product
            elif mode == "add":
                acc[rows, hid] += product
            else:
                pre_ref[rows, hid] = ((acc[rows, hid] + product) * slope[rows, hid]).astype(jnp.bfloat16)
            return carry

        lax.fori_loop(0, HID // 256, body, 0)

    whole = pl.ds(0, TOK)
    own_copy.wait()
    s_own.wait_recv()
    weight_grad_pair(z)
    loads[0].wait()
    pre_product(z, 0, whole, "first")
    loads[3].start()
    z_own[0].wait_recv()
    z_fwd[0].start()
    s_fwd[0].start()
    z_own[1].wait_recv()
    z_fwd[1].start()
    s_fwd[1].start()
    loads[1].wait()
    loads[2].wait()
    s_fwd[0].wait_recv()
    pre_product(z_left, 1, h0, "add")
    s_fwd[1].wait_recv()
    pre_product(z_right, 2, h1, "add")
    z_own[2].wait_recv()
    s_fwd[2].start()
    z_own[3].wait_recv()
    s_fwd[3].start()
    s_fwd[2].wait_recv()
    weight_grad_pair(z_left)
    s_fwd[3].wait_recv()
    weight_grad_pair(z_right)
    pre_product(z_left, 1, h1, "add")
    pre_product(z_right, 2, h0, "add")
    z_fwd[0].wait_recv()
    s_fwd[4].start()
    z_fwd[1].wait_recv()
    s_fwd[5].start()
    weight_grad_part(z_far, core)
    s_fwd[4].wait_recv()
    s_fwd[5].wait_recv()
    weight_grad_part(z_far, 1 - core)

    scale = 1.0 / math.sqrt(TOK * 16)

    def gather(half, q, row, count):
        groups = count // GROUP

        def body(n, carry):
            p = n // groups
            at = pl.multiple_of(row + (n - p * groups) * GROUP, GROUP)
            ry, rx = (p, q) if half == 0 else (q, p)
            first = (ry * 4 + rx) * KEEP + at
            buf = lax.rem(n, 2)
            for s in range(GROUP):
                stage[buf, pl.ds(s, 1), :] = wg[pl.ds(src_ref[first + s], 1), :]
            send[ry, rx, pl.ds(at, GROUP), :] = (stage[buf] * scale).astype(jnp.bfloat16)
            return carry

        lax.fori_loop(0, 4 * groups, body, 0)

    def many(buf, half, q, row, count):
        return buf.at[:, q, pl.ds(row, count)] if half == 0 else buf.at[q, :, pl.ds(row, count)]

    def one(buf, half, q, row, count):
        return buf.at[q, x, pl.ds(row, count)] if half == 0 else buf.at[y, q, pl.ds(row, count)]

    bufs = (
        ((f1a, l1a, r1a), (f2a, l2a, r2a)),
        ((f1b, l1b, r1b), (f2b, l2b, r2b)),
    )

    def scatter_copies(half, level):
        low, a, b = SPLIT[half]
        fwd, left, right = bufs[half][level]
        along_x = half == level
        devices = dev_x if along_x else dev_y
        here = x if along_x else y
        pick = many if level == 0 else one
        base = 20 * half + 6 * level

        def sub(buf, row, count):
            return buf.at[:, pl.ds(row, count)] if level == 0 else buf.at[pl.ds(row, count)]

        def copy(n, q, row, count, dst, way):
            return remote(
                pick(send, half, q, low + row, count), sub(dst, row, count),
                d_send.at[base + n], d_recv.at[base + n], devices[way],
            )

        nxt, prv, far = step(here, 1), step(here, -1), step(here, 2)
        return (
            copy(0, far, 0, a, fwd, 0),
            copy(1, far, a, b, fwd, 1),
            copy(2, nxt, a, b, left, 0),
            copy(3, prv, 0, a, right, 1),
            copy(4, nxt, 0, a, left, 0),
            copy(5, prv, a, b, right, 1),
        ), (nxt, prv, far, here)

    def add_forward(half, level, places, way):
        low, a, b = SPLIT[half]
        fwd = bufs[half][level][0]
        row, count = (0, a) if way == 0 else (a, b)
        q = places[way]
        if level == 0:
            def body(p, carry):
                ry, rx = (p, q) if half == 0 else (q, p)
                rows = pl.ds(low + row, count)
                send[ry, rx, rows, :] = (
                    send[ry, rx, rows, :].astype(jnp.float32) + fwd[p, pl.ds(row, count), :].astype(jnp.float32)
                ).astype(jnp.bfloat16)
                return carry

            lax.fori_loop(0, 4, body, 0)
        else:
            ry, rx = (q, x) if half == 0 else (y, q)
            rows = pl.ds(low + row, count)
            send[ry, rx, rows, :] = (
                send[ry, rx, rows, :].astype(jnp.float32) + fwd[pl.ds(row, count), :].astype(jnp.float32)
            ).astype(jnp.bfloat16)

    def add_own(half, level):
        low, a, b = SPLIT[half]
        _, left, right = bufs[half][level]
        rows = pl.ds(low, a + b)
        if level == 0:
            def body(p, carry):
                ry, rx = (p, x) if half == 0 else (y, p)
                send[ry, rx, rows, :] = (
                    send[ry, rx, rows, :].astype(jnp.float32)
                    + left[p].astype(jnp.float32)
                    + right[p].astype(jnp.float32)
                ).astype(jnp.bfloat16)
                return carry

            lax.fori_loop(0, 4, body, 0)
        else:
            out_ref[y, x, rows, :] = (
                send[y, x, rows, :].astype(jnp.float32)
                + left[...].astype(jnp.float32)
                + right[...].astype(jnp.float32)
            ).astype(jnp.bfloat16)

    first = [scatter_copies(half, 0) for half in range(2)]
    second = [scatter_copies(half, 1) for half in range(2)]
    for half in range(2):
        low, a, b = SPLIT[half]
        copies, (nxt, prv, far, here) = first[half]
        gather(half, far, low, a + b)
        copies[0].start()
        copies[1].start()
    for half in range(2):
        low, a, b = SPLIT[half]
        copies, (nxt, prv, far, here) = first[half]
        gather(half, nxt, low + a, b)
        copies[2].start()
        gather(half, prv, low, a)
        copies[3].start()
    for half in range(2):
        low, a, b = SPLIT[half]
        copies, (nxt, prv, far, here) = first[half]
        gather(half, nxt, low, a)
        copies[0].wait_recv()
        add_forward(half, 0, (nxt, prv), 0)
        copies[4].start()
        gather(half, prv, low + a, b)
        copies[1].wait_recv()
        add_forward(half, 0, (nxt, prv), 1)
        copies[5].start()
    for half in range(2):
        low, a, b = SPLIT[half]
        gather(half, first[half][1][3], low, a + b)

    loads[3].wait()
    pre_product(z_far, 0, whole, "last")

    for half in range(2):
        for n in range(2, 6):
            first[half][0][n].wait_recv()
        add_own(half, 0)
        for n in range(4):
            second[half][0][n].start()
    for half in range(2):
        copies, (nxt, prv, far, here) = second[half]
        for way in range(2):
            copies[way].wait_recv()
            add_forward(half, 1, (nxt, prv), way)
            copies[4 + way].start()

    def gather_copies(half, level):
        low, a, b = SPLIT[half]
        along_x = half == 1 - level
        devices = dev_x if along_x else dev_y
        here = x if along_x else y
        pick = one if level == 0 else many
        base = 20 * half + 12 + 4 * level

        def copy(n, q, row, count, way):
            part = pick(out_ref, half, q, low + row, count)
            return remote(part, part, d_send.at[base + n], d_recv.at[base + n], devices[way])

        nxt, prv = step(here, 1), step(here, -1)
        return (
            copy(0, here, 0, a + b, 0),
            copy(1, here, 0, a + b, 1),
            copy(2, prv, 0, a, 0),
            copy(3, nxt, a, b, 1),
        )

    third = [gather_copies(half, 0) for half in range(2)]
    fourth = [gather_copies(half, 1) for half in range(2)]
    for half in range(2):
        for n in range(2, 6):
            second[half][0][n].wait_recv()
        add_own(half, 1)
        third[half][0].start()
        third[half][1].start()
    for half in range(2):
        for n in range(2):
            third[half][n].wait_recv()
            third[half][2 + n].start()
    for half in range(2):
        third[half][2].wait_recv()
        third[half][3].wait_recv()
        fourth[half][0].start()
        fourth[half][1].start()
    for half in range(2):
        for n in range(2):
            fourth[half][n].wait_recv()
            fourth[half][2 + n].start()
    for half in range(2):
        fourth[half][2].wait_recv()
        fourth[half][3].wait_recv()

    for copy in (*z_own, s_own, *z_fwd, *s_fwd):
        copy.wait_send()
    for half in range(2):
        for copy in (*first[half][0], *second[half][0], *third[half], *fourth[half]):
            copy.wait_send()


def fused(u, grad_part, weights, source):
    rows_a = SPLIT[0][1] + SPLIT[0][2]
    rows_b = SPLIT[1][1] + SPLIT[1][2]
    big = [pltpu.VMEM((4, rows, LANES), jnp.bfloat16) for rows in (rows_a, rows_b) for _ in range(3)]
    small = [pltpu.VMEM((rows, LANES), jnp.bfloat16) for rows in (rows_a, rows_b) for _ in range(3)]
    vmem = pl.BlockSpec(memory_space=pltpu.VMEM)
    hbm = pl.BlockSpec(memory_space=pl.ANY)
    return pl.pallas_call(
        kernel,
        out_shape=(
            jax.ShapeDtypeStruct((TOK, HID), jnp.bfloat16),
            jax.ShapeDtypeStruct((4, 4, KEEP, LANES), jnp.bfloat16),
        ),
        in_specs=[vmem, hbm, hbm, pl.BlockSpec(memory_space=pltpu.SMEM)],
        out_specs=(vmem, vmem),
        scratch_shapes=[
            pltpu.VMEM((NBLK + GROUP, LANES), jnp.float32),
            pltpu.VMEM((3, HID, PAIR), jnp.bfloat16),
            pltpu.VMEM((4, TOK, PAIR), jnp.bfloat16),
            pltpu.VMEM((HID, TOK), jnp.bfloat16),
            pltpu.VMEM((TOK, HID), jnp.float32),
            pltpu.VMEM((TOK, HID), jnp.float32),
            pltpu.VMEM((4, 4, KEEP, LANES), jnp.bfloat16),
            pltpu.VMEM((2, GROUP, LANES), jnp.float32),
            *big,
            *small,
            pltpu.SemaphoreType.DMA((1,)),
            pltpu.SemaphoreType.DMA((4,)),
            pltpu.SemaphoreType.DMA((6,)),
            pltpu.SemaphoreType.DMA((6,)),
            pltpu.SemaphoreType.DMA((7,)),
            pltpu.SemaphoreType.DMA((7,)),
            pltpu.SemaphoreType.DMA((40,)),
            pltpu.SemaphoreType.DMA((40,)),
        ],
        compiler_params=pltpu.CompilerParams(
            collective_id=0, has_side_effects=True, vmem_limit_bytes=62 * 1024 * 1024
        ),
        cost_estimate=pl.CostEstimate(
            flops=4 * TOK * HID * WIDTH, bytes_accessed=20_000_000, transcendentals=2 * TOK * HID
        ),
    )(u, grad_part, weights, source)


def local(
    inner_before_nonlinear,
    layer_exit_derivative,
    contract_weights,
    copy_tile_indicator,
    span_opening_tile,
    remaining_tile_flags,
):
    source = slot_sources(remaining_tile_flags[0], copy_tile_indicator[0, 0], span_opening_tile)
    pre_grad, sums = fused(inner_before_nonlinear, layer_exit_derivative, contract_weights, source)
    return (pre_grad, sums.reshape(1, 16 * KEEP, LANES).astype(jnp.float32))


def solution(mesh):
    in_specs = (
        P("dp", "mp"),
        P("dp", "mp"),
        P("mp", None),
        P("dp", "mp", None),
        P(),
        P("mp", None),
    )
    out_specs = (P("dp", "mp"), P("mp", None, None))
    return jax.shard_map(local, mesh=mesh, in_specs=in_specs, out_specs=out_specs, check_vma=False)
```

```python
import functools
import math

import jax
import jax.numpy as jnp
from jax import lax
from jax.experimental import pallas as pl
from jax.experimental.pallas import tpu as pltpu
from jax.sharding import PartitionSpec as P

half_root = 0.7071067811865476
inv_root_tau = 0.3989422804014327
MESH = pl.DeviceIdType.MESH

TOK = 512
HID = 1280
WIDTH = 5120
PART = 640
PAIR = 2 * PART
LANES = 128
COLS = WIDTH // LANES
NBLK = HID * COLS
KEEP = 400
HALF = TOK // 2
GROUP = 16
ROWS = NBLK // LANES
ROWS_PAD = 448
WINDOW = 48
SLOTS = 512
CUT = 384
SPLIT = ((0, 112, 96), (208, 96, 96))


def index_kernel(flag_ref, copied_ref, start_ref, src_ref, flags, copied, within, upto, before, opening):
    flags[pl.ds(0, ROWS), :] = flag_ref[...]
    copied[pl.ds(0, ROWS), :] = copied_ref[...].astype(jnp.float32)
    pad = pl.ds(ROWS, ROWS_PAD - ROWS)
    flags[pad, :] = jnp.zeros((ROWS_PAD - ROWS, LANES), jnp.int32)
    copied[pad, :] = jnp.zeros((ROWS_PAD - ROWS, LANES), jnp.float32)

    def iota(shape, dim):
        return lax.broadcasted_iota(jnp.int32, shape, dim)

    square = (LANES, LANES)
    flag_bf = flags[...].astype(jnp.float32).astype(jnp.bfloat16)
    tri = jnp.where(iota(square, 0) <= iota(square, 1), 1.0, 0.0).astype(jnp.bfloat16)
    within[...] = jnp.dot(flag_bf, tri, preferred_element_type=jnp.float32)
    totals = jnp.dot(flag_bf, jnp.ones(square, jnp.bfloat16), preferred_element_type=jnp.float32)
    tall = (ROWS_PAD, ROWS_PAD)
    tri = jnp.where(iota(tall, 0) >= iota(tall, 1), 1.0, 0.0).astype(jnp.bfloat16)
    sums = jnp.dot(tri, totals.astype(jnp.bfloat16), preferred_element_type=jnp.float32)
    upto[...] = sums
    before[...] = sums - totals
    for o in range(17):
        start = start_ref[o]
        row = pl.ds(lax.shift_right_logical(start, 7), 1)
        inside = jnp.where(iota((1, LANES), 1) < lax.bitwise_and(start, 127), flags[row, :], 0).astype(jnp.float32)
        opening[pl.ds(o, 1), :] = before[row, :] + jnp.sum(inside, axis=1, keepdims=True)

    def wide(v):
        return jnp.concatenate([v] * (SLOTS // LANES), axis=1)

    def sources(o):
        row0 = pl.multiple_of(lax.bitwise_and(lax.shift_right_logical(start_ref[o], 7), -8), 8)
        rows = pl.ds(row0, WINDOW)
        target = wide(opening[pl.ds(o, 1), :]) + iota((1, SLOTS), 1).astype(jnp.float32)
        limit = wide(opening[pl.ds(o + 1, 1), :])
        ends = wide(upto[rows, :])
        passed = ends <= target
        count = jnp.sum(jnp.where(passed, 1.0, 0.0), axis=0, keepdims=True)
        last = jnp.max(jnp.where(passed, ends, wide(before[pl.ds(row0, 1), :])), axis=0, keepdims=True)
        pick = jnp.where(iota((WINDOW, SLOTS), 0).astype(jnp.float32) == count, 1.0, 0.0).astype(jnp.bfloat16)

        def lookup(table):
            return lax.dot_general(
                table.astype(jnp.bfloat16), pick, (((0,), (0,)), ((), ())), preferred_element_type=jnp.float32
            )

        at = jnp.sum(jnp.where(lookup(within[rows, :]) <= target - last, 1.0, 0.0), axis=0, keepdims=True)
        here = iota((LANES, SLOTS), 0).astype(jnp.float32) == at
        kept = jnp.sum(
            jnp.where(here, lookup(copied[rows, :]), 0.0), axis=0, keepdims=True
        )
        block = (count + row0.astype(jnp.float32)) * LANES + at
        hid = jnp.floor((block + 0.5) * (1.0 / COLS))
        source = (block - hid * COLS) * HID + hid
        source = jnp.where((target < limit) & (kept > 0.5), source, float(NBLK))
        src_ref[:, pl.ds(o * SLOTS, SLOTS)] = source.astype(jnp.int32)

    for o in range(16):
        sources(o)


def slot_sources(flags, copied, starts):
    vmem = pl.BlockSpec(memory_space=pltpu.VMEM)
    table = pltpu.VMEM((ROWS_PAD, LANES), jnp.float32)
    return pl.pallas_call(
        index_kernel,
        out_shape=jax.ShapeDtypeStruct((1, 16 * SLOTS), jnp.int32),
        in_specs=[vmem, vmem, pl.BlockSpec(memory_space=pltpu.SMEM)],
        out_specs=vmem,
        scratch_shapes=[
            pltpu.VMEM((ROWS_PAD, LANES), jnp.int32),
            table,
            table,
            table,
            table,
            pltpu.VMEM((24, LANES), jnp.float32),
        ],
    )(flags, copied, starts)


def kernel(
    u_ref, g_ref, w_ref, src_ref,
    pre_out, out_ref,
    wg, wbuf, grad, act_t, slope, acc, send_a, send_b, u_buf, pre_ref,
    f1a, l1a, r1a, f1b, l1b, r1b, f2a, l2a, r2a, f2b, l2b, r2b,
    local_sem, w_sem, z_send, z_recv, s_send, s_recv, d_send, d_recv,
):
    dp = lax.axis_index("dp")
    mp = lax.axis_index("mp")
    y, x = dp // 4, lax.rem(dp, 4)
    z, core = mp // 2, lax.rem(mp, 2)

    def step(p, d):
        return lax.rem(p + d + 4, 4)

    z_right, z_left, z_far = step(z, 1), step(z, -1), step(z, 2)
    dev_z = ((dp, z_right * 2 + core), (dp, z_left * 2 + core))
    dev_sib = (dp, z * 2 + 1 - core)
    dev_x = ((y * 4 + step(x, 1), mp), (y * 4 + step(x, -1), mp))
    dev_y = ((step(y, 1) * 4 + x, mp), (step(y, -1) * 4 + x, mp))

    barrier = pltpu.get_barrier_semaphore()
    peers = (*dev_z, dev_sib, *dev_x, *dev_y, (y * 4 + step(x, 2), mp), (step(y, 2) * 4 + x, mp))
    for peer in peers:
        pl.semaphore_signal(barrier, inc=1, device_id=peer, device_id_type=MESH)

    def w_load(zp, slot, sem):
        cols = pl.ds(pl.multiple_of(zp * PAIR, LANES), PAIR)
        return pltpu.make_async_copy(w_ref.at[:, cols], wbuf.at[slot], w_sem.at[sem])

    mine = pl.ds(pl.multiple_of(core * PART, LANES), PART)
    other = pl.ds(pl.multiple_of((1 - core) * PART, LANES), PART)
    own_copy = pltpu.make_async_copy(g_ref, grad.at[z, :, mine], local_sem.at[0])
    u_copy = pltpu.make_async_copy(u_ref, u_buf, local_sem.at[1])
    u_copy.start()
    own_copy.start()
    loads = [w_load(z, 0, 0), w_load(z_left, 1, 1), w_load(z_right, 2, 2), w_load(z_far, 0, 3)]
    pl.semaphore_wait(barrier, len(peers))

    h0, h1 = pl.ds(0, HALF), pl.ds(HALF, HALF)

    def remote(src, dst, s_sem, r_sem, device):
        return pltpu.make_async_remote_copy(
            src_ref=src, dst_ref=dst, send_sem=s_sem, recv_sem=r_sem, device_id=device, device_id_type=MESH
        )

    def z_copy(n, src, zp, rows, way):
        return remote(src, grad.at[zp, rows, mine], z_send.at[n], z_recv.at[n], dev_z[way])

    def piece(zp, rows, col, width):
        return grad.at[zp, rows, pl.ds(pl.multiple_of(core * PART + col, LANES), width)]

    def z_pass(n, zp, rows, col, width, way):
        part = piece(zp, rows, col, width)
        return remote(part, part, z_send.at[n], z_recv.at[n], dev_z[way])

    def s_copy(n, zp, rows, col=0, width=PART):
        part = piece(zp, rows, col, width)
        return remote(part, part, s_send.at[n], s_recv.at[n], dev_sib)

    z_own = [
        z_copy(0, g_ref.at[h0], z, h0, 0),
        z_copy(1, g_ref.at[h1], z, h1, 1),
        z_copy(2, g_ref.at[h1], z, h1, 0),
        z_copy(3, g_ref.at[h0], z, h0, 1),
    ]
    s_own = remote(g_ref, grad.at[z, :, mine], s_send.at[0], s_recv.at[0], dev_sib)
    z_own[0].start()
    z_own[1].start()
    s_own.start()
    z_fwd = [
        z_pass(4, z_left, h0, 0, CUT, 0),
        z_pass(5, z_right, h1, 0, CUT, 1),
        z_pass(6, z_left, h0, CUT, PART - CUT, 0),
        z_pass(7, z_right, h1, CUT, PART - CUT, 1),
    ]
    s_fwd = [
        s_copy(1, z_left, h0),
        s_copy(2, z_right, h1),
        s_copy(3, z_left, h1),
        s_copy(4, z_right, h0),
        s_copy(5, z_far, h0, 0, CUT),
        s_copy(6, z_far, h1, 0, CUT),
        s_copy(7, z_far, h0, CUT, PART - CUT),
        s_copy(8, z_far, h1, CUT, PART - CUT),
    ]

    wg[pl.ds(NBLK, GROUP), :] = jnp.zeros((GROUP, LANES), jnp.float32)

    u_copy.wait()
    for load in loads[:3]:
        load.start()

    def gelu(n, carry):
        tok = pl.ds(pl.multiple_of(lax.rem(n, 4) * LANES, LANES), LANES)
        hid = pl.ds(pl.multiple_of((n // 4) * LANES, LANES), LANES)
        values = u_buf[tok, hid].astype(jnp.float32)
        cdf = 0.5 * (1.0 + lax.erf(values * half_root))
        density = jnp.exp(-0.5 * values * values) * inv_root_tau
        act_t[hid, tok] = (values * cdf).T.astype(jnp.bfloat16)
        slope[tok, hid] = cdf + values * density
        return carry

    lax.fori_loop(0, 4 * (HID // LANES), gelu, 0)

    def weight_grad(zp, n, part_cols, width):
        cols = pl.ds(pl.multiple_of(part_cols + n * width, LANES), width)
        first = zp * (PAIR // LANES) + (part_cols + n * width) // LANES
        for half in range(2):
            product = jnp.dot(
                act_t[pl.ds(half * PART, PART), :], grad[zp, :, cols], preferred_element_type=jnp.float32
            )
            for c in range(width // LANES):
                row = pl.multiple_of((first + c) * HID + half * PART, LANES)
                wg[pl.ds(row, PART), :] = product[:, c * LANES : (c + 1) * LANES]

    def weight_grad_pair(zp):
        def body(n, carry):
            weight_grad(zp, n, 0, 256)
            return carry

        lax.fori_loop(0, PAIR // 256, body, 0)

    def pre_product(zp, slot, rows, mode):
        def body(n, carry):
            hid = pl.ds(pl.multiple_of(n * 256, LANES), 256)
            product = lax.dot_general(
                grad[zp, rows, :], wbuf[slot, hid, :], (((1,), (1,)), ((), ())),
                preferred_element_type=jnp.float32,
            )
            if mode == "first":
                acc[rows, hid] = product
            elif mode == "add":
                acc[rows, hid] += product
            else:
                pre_ref[rows, hid] = ((acc[rows, hid] + product) * slope[rows, hid]).astype(jnp.bfloat16)
            return carry

        lax.fori_loop(0, HID // 256, body, 0)

    whole = pl.ds(0, TOK)
    own_copy.wait()
    s_own.wait_recv()
    weight_grad_pair(z)
    z_own[2].start()
    z_own[3].start()
    loads[0].wait()
    pre_product(z, 0, whole, "first")
    loads[3].start()
    z_own[0].wait_recv()
    s_fwd[0].start()
    z_own[1].wait_recv()
    s_fwd[1].start()
    loads[1].wait()
    loads[2].wait()
    s_fwd[0].wait_recv()
    pre_product(z_left, 1, h0, "add")
    s_fwd[1].wait_recv()
    pre_product(z_right, 2, h1, "add")
    z_fwd[0].start()
    z_fwd[1].start()
    z_own[2].wait_recv()
    s_fwd[2].start()
    z_own[3].wait_recv()
    s_fwd[3].start()
    z_fwd[2].start()
    z_fwd[3].start()
    s_fwd[2].wait_recv()
    weight_grad_pair(z_left)
    z_fwd[0].wait_recv()
    s_fwd[4].start()
    z_fwd[1].wait_recv()
    s_fwd[5].start()
    s_fwd[3].wait_recv()
    weight_grad_pair(z_right)
    weight_grad(z_far, 0, core * PART, CUT)
    for way in range(2):
        s_fwd[4 + way].wait_recv()
    weight_grad(z_far, 0, (1 - core) * PART, CUT)
    for way in range(2):
        z_fwd[2 + way].wait_recv()
        s_fwd[6 + way].start()
    weight_grad(z_far, 0, core * PART + CUT, PART - CUT)
    for way in range(2):
        s_fwd[6 + way].wait_recv()
    weight_grad(z_far, 0, (1 - core) * PART + CUT, PART - CUT)

    scale = 1.0 / math.sqrt(TOK * 16)
    FAR, NEXT, PREV, OWN = range(4)
    SHIFT = (2, 1, -1, 0)
    parts = ((FAR, NEXT), (PREV, OWN))
    send = (send_a, send_b)
    bufs = (
        ((f1a, l1a, r1a), (f2a, l2a, r2a)),
        ((f1b, l1b, r1b), (f2b, l2b, r2b)),
    )

    def axis(half, level):
        along_x = half == level
        places = tuple(step(x if along_x else y, shift) for shift in SHIFT)
        devices = tuple((y * 4 + p, mp) if along_x else (p * 4 + x, mp) for p in places)
        return places, devices

    def gather(half, part, place, row, count):
        low = SPLIT[half][0]
        groups = count // GROUP
        one = axis(half, 0)[0][place]
        for second in parts[part]:
            two = axis(half, 1)[0][second]
            region = two * 4 + one if half == 0 else one * 4 + two

            def body(n, carry):
                at = pl.multiple_of(row + n * GROUP, GROUP)
                first = region * SLOTS + low + at
                taken = [wg[pl.ds(src_ref[0, first + s], 1), :] for s in range(GROUP)]
                send[half][second, place, pl.ds(at, GROUP), :] = (
                    jnp.concatenate(taken, axis=0) * scale
                ).astype(jnp.bfloat16)
                return carry

            lax.fori_loop(0, groups, body, 0)

    def scatter_first(half, part):
        _, a, b = SPLIT[half]
        fwd, left, right = bufs[half][0]
        devices = axis(half, 0)[1]
        lead = pl.ds(2 * part, 2)
        base = 32 * half + 6 * part

        def copy(n, place, row, count, dst, way):
            return remote(
                send[half].at[lead, place, pl.ds(row, count)], dst.at[lead, pl.ds(row, count)],
                d_send.at[base + n], d_recv.at[base + n], devices[way],
            )

        return (
            copy(0, FAR, 0, a, fwd, NEXT),
            copy(1, FAR, a, b, fwd, PREV),
            copy(2, NEXT, a, b, left, NEXT),
            copy(3, PREV, 0, a, right, PREV),
            copy(4, NEXT, 0, a, left, NEXT),
            copy(5, PREV, a, b, right, PREV),
        )

    def scatter_second(half):
        devices = axis(half, 1)[1]
        far, left, right = bufs[half][1]

        def copy(n, place, dst):
            return remote(
                send[half].at[place, OWN], dst,
                d_send.at[32 * half + 12 + n], d_recv.at[32 * half + 12 + n], devices[place],
            )

        return (copy(0, FAR, far), copy(1, NEXT, left), copy(2, PREV, right))

    def add_forward(half, part, way):
        _, a, b = SPLIT[half]
        fwd = bufs[half][0][0]
        row, count, place = ((0, a, NEXT), (a, b, PREV))[way]
        rows = pl.ds(row, count)
        for second in parts[part]:
            send[half][second, place, rows, :] = (
                send[half][second, place, rows, :].astype(jnp.float32) + fwd[second, rows, :].astype(jnp.float32)
            ).astype(jnp.bfloat16)

    def add_first(half, part):
        _, left, right = bufs[half][0]
        for second in parts[part]:
            send[half][second, OWN] = (
                send[half][second, OWN].astype(jnp.float32)
                + left[second].astype(jnp.float32)
                + right[second].astype(jnp.float32)
            ).astype(jnp.bfloat16)

    def add_second(half):
        low, a, b = SPLIT[half]
        far, left, right = bufs[half][1]
        out_ref[y, x, pl.ds(low, a + b), :] = (
            send[half][OWN, OWN].astype(jnp.float32)
            + far[...].astype(jnp.float32)
            + left[...].astype(jnp.float32)
            + right[...].astype(jnp.float32)
        ).astype(jnp.bfloat16)

    first = [[scatter_first(half, part) for part in range(2)] for half in range(2)]
    second = [scatter_second(half) for half in range(2)]

    def start_far(half, part):
        gather(half, part, FAR, 0, SPLIT[half][1] + SPLIT[half][2])
        first[half][part][0].start()
        first[half][part][1].start()

    def start_near(half, part):
        _, a, b = SPLIT[half]
        gather(half, part, NEXT, a, b)
        first[half][part][2].start()
        gather(half, part, PREV, 0, a)
        first[half][part][3].start()

    def gather_rest(half, part):
        _, a, b = SPLIT[half]
        gather(half, part, NEXT, 0, a)
        gather(half, part, PREV, a, b)
        gather(half, part, OWN, 0, a + b)

    def pass_on(half, part):
        for way in range(2):
            first[half][part][way].wait_recv()
            add_forward(half, part, way)
            first[half][part][4 + way].start()

    for part in range(2):
        for half in range(2):
            start_far(half, part)
    for half in range(2):
        start_near(half, 0)
    for part in range(2):
        for half in range(2):
            gather_rest(half, part)
    pre_product(z_left, 1, h1, "add")
    for half in range(2):
        pass_on(half, 0)
    for half in range(2):
        start_near(half, 1)
    for half in range(2):
        pass_on(half, 1)
    pre_product(z_right, 2, h0, "add")
    for part in range(2):
        for half in range(2):
            for n in range(2, 6):
                first[half][part][n].wait_recv()
            add_first(half, part)
            for place in parts[part]:
                if place != OWN:
                    second[half][place].start()

    def spread_copies(half):
        low, a, b = SPLIT[half]
        devices = axis(half, 1)[1]
        part = out_ref.at[y, x, pl.ds(low, a + b)]
        base = 32 * half + 15
        return [
            remote(part, part, d_send.at[base + place], d_recv.at[base + place], devices[place])
            for place in (FAR, NEXT, PREV)
        ]

    def region_copies(half, place):
        low, a, b = SPLIT[half]
        places, devices = axis(half, 0)
        q = axis(half, 1)[0][place]
        base = 32 * half + 18 + (0, 3, 7, 11)[place]

        def copy(n, column, row, count, way):
            rows = pl.ds(low + row, count)
            part = out_ref.at[q, column, rows] if half == 0 else out_ref.at[column, q, rows]
            return remote(part, part, d_send.at[base + n], d_recv.at[base + n], devices[way])

        near = (copy(0, places[OWN], 0, a + b, NEXT), copy(1, places[OWN], 0, a + b, PREV))
        if place in (FAR, OWN):
            return (*near, copy(2, places[OWN], 0, a + b, FAR))
        return (*near, copy(2, places[PREV], 0, a, NEXT), copy(3, places[NEXT], a, b, PREV))

    third = [spread_copies(half) for half in range(2)]
    fourth = [[region_copies(half, place) for place in range(4)] for half in range(2)]

    def send_region(half, place):
        for copy in fourth[half][place][: 3 if place in (FAR, OWN) else 2]:
            copy.start()

    for half in range(2):
        for copy in second[half]:
            copy.wait_recv()
        add_second(half)
        for place in (NEXT, PREV, FAR):
            third[half][place].start()
    for half in range(2):
        send_region(half, OWN)
    loads[3].wait()
    pre_product(z_far, 0, whole, "last")
    pre_copy = pltpu.make_async_copy(pre_ref, pre_out, local_sem.at[2])
    pre_copy.start()
    for place, arrived in ((NEXT, PREV), (PREV, NEXT), (FAR, FAR)):
        for half in range(2):
            third[half][arrived].wait_recv()
            send_region(half, place)
    for place in (NEXT, PREV):
        for half in range(2):
            for way in range(2):
                fourth[half][place][way].wait_recv()
                fourth[half][place][2 + way].start()
    for half in range(2):
        for place in (OWN, FAR):
            for copy in fourth[half][place]:
                copy.wait_recv()
        for place in (NEXT, PREV):
            for copy in fourth[half][place][2:]:
                copy.wait_recv()
    pre_copy.wait()

    for copy in (*z_own, s_own, *z_fwd, *s_fwd):
        copy.wait_send()
    for half in range(2):
        groups = (*first[half], second[half], third[half], *fourth[half])
        for copy in (c for group in groups for c in group):
            copy.wait_send()


def fused(u, grad_part, weights, source):
    rows_a = SPLIT[0][1] + SPLIT[0][2]
    rows_b = SPLIT[1][1] + SPLIT[1][2]
    big = [pltpu.VMEM((4, rows, LANES), jnp.bfloat16) for rows in (rows_a, rows_b) for _ in range(3)]
    small = [pltpu.VMEM((rows, LANES), jnp.bfloat16) for rows in (rows_a, rows_b) for _ in range(3)]
    vmem = pl.BlockSpec(memory_space=pltpu.VMEM)
    hbm = pl.BlockSpec(memory_space=pl.ANY)
    return pl.pallas_call(
        kernel,
        out_shape=(
            jax.ShapeDtypeStruct((TOK, HID), jnp.bfloat16),
            jax.ShapeDtypeStruct((4, 4, KEEP, LANES), jnp.bfloat16),
        ),
        in_specs=[hbm, hbm, hbm, pl.BlockSpec(memory_space=pltpu.SMEM)],
        out_specs=(hbm, vmem),
        scratch_shapes=[
            pltpu.VMEM((NBLK + GROUP, LANES), jnp.float32),
            pltpu.VMEM((3, HID, PAIR), jnp.bfloat16),
            pltpu.VMEM((4, TOK, PAIR), jnp.bfloat16),
            pltpu.VMEM((HID, TOK), jnp.bfloat16),
            pltpu.VMEM((TOK, HID), jnp.float32),
            pltpu.VMEM((TOK, HID), jnp.float32),
            pltpu.VMEM((4, 4, rows_a, LANES), jnp.bfloat16),
            pltpu.VMEM((4, 4, rows_b, LANES), jnp.bfloat16),
            pltpu.VMEM((TOK, HID), jnp.bfloat16),
            pltpu.VMEM((TOK, HID), jnp.bfloat16),
            *big,
            *small,
            pltpu.SemaphoreType.DMA((3,)),
            pltpu.SemaphoreType.DMA((4,)),
            pltpu.SemaphoreType.DMA((8,)),
            pltpu.SemaphoreType.DMA((8,)),
            pltpu.SemaphoreType.DMA((9,)),
            pltpu.SemaphoreType.DMA((9,)),
            pltpu.SemaphoreType.DMA((64,)),
            pltpu.SemaphoreType.DMA((64,)),
        ],
        compiler_params=pltpu.CompilerParams(
            collective_id=0, has_side_effects=True, vmem_limit_bytes=57 * 1024 * 1024
        ),
        cost_estimate=pl.CostEstimate(
            flops=4 * TOK * HID * WIDTH, bytes_accessed=20_000_000, transcendentals=2 * TOK * HID
        ),
    )(u, grad_part, weights, source)


FINISH = 4


def finish_kernel(pre_ref, sums_ref, pre_out, sums_out, pre_buf, sums_buf, wide_buf, in_sem, out_sem):
    slots = 16 * KEEP // FINISH
    pre_in = pltpu.make_async_copy(pre_ref, pre_buf, in_sem.at[FINISH])
    pre_back = pltpu.make_async_copy(pre_buf, pre_out, out_sem.at[FINISH])
    parts = [pl.ds(n * slots, slots) for n in range(FINISH)]
    loads = [pltpu.make_async_copy(sums_ref.at[part], sums_buf.at[part], in_sem.at[n]) for n, part in enumerate(parts)]
    stores = [pltpu.make_async_copy(wide_buf.at[part], sums_out.at[part], out_sem.at[n]) for n, part in enumerate(parts)]
    for load in loads:
        load.start()
    pre_in.start()
    for part, load, store in zip(parts, loads, stores):
        load.wait()
        wide_buf[part, :] = sums_buf[part, :].astype(jnp.float32)
        store.start()
    pre_in.wait()
    pre_back.start()
    for store in stores:
        store.wait()
    pre_back.wait()


def finish(pre_grad, sums):
    hbm = pl.BlockSpec(memory_space=pltpu.HBM)
    return pl.pallas_call(
        finish_kernel,
        out_shape=(
            jax.ShapeDtypeStruct((TOK, HID), jnp.bfloat16),
            jax.ShapeDtypeStruct((16 * KEEP, LANES), jnp.float32),
        ),
        in_specs=[hbm, hbm],
        out_specs=(hbm, hbm),
        scratch_shapes=[
            pltpu.VMEM((TOK, HID), jnp.bfloat16),
            pltpu.VMEM((16 * KEEP, LANES), jnp.bfloat16),
            pltpu.VMEM((16 * KEEP, LANES), jnp.float32),
            pltpu.SemaphoreType.DMA((FINISH + 1,)),
            pltpu.SemaphoreType.DMA((FINISH + 1,)),
        ],
    )(pre_grad, sums)


def local(
    inner_before_nonlinear,
    layer_exit_derivative,
    contract_weights,
    copy_tile_indicator,
    span_opening_tile,
    remaining_tile_flags,
):
    source = slot_sources(
        remaining_tile_flags.reshape(ROWS, LANES), copy_tile_indicator.reshape(ROWS, LANES), span_opening_tile
    )
    pre_grad, sums = fused(inner_before_nonlinear, layer_exit_derivative, contract_weights, source)
    pre_grad, sums = finish(pre_grad, sums.reshape(16 * KEEP, LANES))
    return (pre_grad, sums[None])


def solution(mesh):
    in_specs = (
        P("dp", "mp"),
        P("dp", "mp"),
        P("mp", None),
        P("dp", "mp", None),
        P(),
        P("mp", None),
    )
    out_specs = (P("dp", "mp"), P("mp", None, None))
    return jax.shard_map(local, mesh=mesh, in_specs=in_specs, out_specs=out_specs, check_vma=False)
```

```python
import functools
import math

import jax
import jax.numpy as jnp
from jax import lax
from jax.experimental import pallas as pl
from jax.experimental.pallas import tpu as pltpu
from jax.sharding import PartitionSpec as P

half_root = 0.7071067811865476
inv_root_tau = 0.3989422804014327
MESH = pl.DeviceIdType.MESH

TOK = 512
HID = 1280
WIDTH = 5120
PART = 640
PAIR = 2 * PART
LANES = 128
COLS = WIDTH // LANES
NBLK = HID * COLS
KEEP = 400
HALF = TOK // 2
GROUP = 16
ROWS = NBLK // LANES
ROWS_PAD = 448
WINDOW = 48
SLOTS = 512
CUT = 256
SPLIT = ((0, 112, 96), (208, 96, 96))


def index_kernel(flag_ref, copied_ref, start_ref, src_ref, flags, within, upto, before, opening):
    flags[pl.ds(0, ROWS), :] = flag_ref[...]
    pad = pl.ds(ROWS, ROWS_PAD - ROWS)
    flags[pad, :] = jnp.zeros((ROWS_PAD - ROWS, LANES), jnp.int32)

    def iota(shape, dim):
        return lax.broadcasted_iota(jnp.int32, shape, dim)

    square = (LANES, LANES)
    flag_bf = flags[...].astype(jnp.float32).astype(jnp.bfloat16)
    tri = jnp.where(iota(square, 0) <= iota(square, 1), 1.0, 0.0).astype(jnp.bfloat16)
    within[...] = jnp.dot(flag_bf, tri, preferred_element_type=jnp.float32) - 64.0
    both = (flag_ref[...] * copied_ref[...]).astype(jnp.float32)
    within[pl.ds(0, ROWS), :] = within[pl.ds(0, ROWS), :] + 0.5 * both
    totals = jnp.dot(flag_bf, jnp.ones(square, jnp.bfloat16), preferred_element_type=jnp.float32)
    tall = (ROWS_PAD, ROWS_PAD)
    tri = jnp.where(iota(tall, 0) >= iota(tall, 1), 1.0, 0.0).astype(jnp.bfloat16)
    sums = jnp.dot(tri, totals.astype(jnp.bfloat16), preferred_element_type=jnp.float32)
    upto[...] = sums
    before[...] = sums - totals
    for o in range(17):
        start = start_ref[o]
        row = pl.ds(lax.shift_right_logical(start, 7), 1)
        inside = jnp.where(iota((1, LANES), 1) < lax.bitwise_and(start, 127), flags[row, :], 0).astype(jnp.float32)
        opening[pl.ds(o, 1), :] = before[row, :] + jnp.sum(inside, axis=1, keepdims=True)

    def wide(v):
        return jnp.concatenate([v] * (SLOTS // LANES), axis=1)

    def sources(o):
        row0 = pl.multiple_of(lax.bitwise_and(lax.shift_right_logical(start_ref[o], 7), -8), 8)
        rows = pl.ds(row0, WINDOW)
        target = wide(opening[pl.ds(o, 1), :]) + iota((1, SLOTS), 1).astype(jnp.float32)
        limit = wide(opening[pl.ds(o + 1, 1), :])
        ends = wide(upto[rows, :])
        passed = ends <= target
        count = jnp.sum(jnp.where(passed, 1.0, 0.0), axis=0, keepdims=True)
        last = jnp.max(jnp.where(passed, ends, wide(before[pl.ds(row0, 1), :])), axis=0, keepdims=True)
        pick = jnp.where(iota((WINDOW, SLOTS), 0).astype(jnp.float32) == count, 1.0, 0.0).astype(jnp.bfloat16)

        found = lax.dot_general(
            within[rows, :].astype(jnp.bfloat16), pick, (((0,), (0,)), ((), ())), preferred_element_type=jnp.float32
        )
        rest = target - last - 64.0
        at = jnp.sum(jnp.where(found < rest + 0.75, 1.0, 0.0), axis=0, keepdims=True)
        kept = jnp.sum(jnp.where(found == rest + 1.5, 1.0, 0.0), axis=0, keepdims=True)
        block = (count + row0.astype(jnp.float32)) * LANES + at
        hid = jnp.floor((block + 0.5) * (1.0 / COLS))
        source = (block - hid * COLS) * HID + hid
        source = jnp.where((target < limit) & (kept > 0.5), source, float(NBLK))
        src_ref[:, pl.ds(o * SLOTS, SLOTS)] = source.astype(jnp.int32)

    for o in range(16):
        sources(o)


def slot_sources(flags, copied, starts):
    vmem = pl.BlockSpec(memory_space=pltpu.VMEM)
    table = pltpu.VMEM((ROWS_PAD, LANES), jnp.float32)
    return pl.pallas_call(
        index_kernel,
        out_shape=jax.ShapeDtypeStruct((1, 16 * SLOTS), jnp.int32),
        in_specs=[vmem, vmem, pl.BlockSpec(memory_space=pltpu.SMEM)],
        out_specs=vmem,
        scratch_shapes=[
            pltpu.VMEM((ROWS_PAD, LANES), jnp.int32),
            table,
            table,
            table,
            pltpu.VMEM((24, LANES), jnp.float32),
        ],
    )(flags, copied, starts)


def kernel(
    u_ref, g_ref, w_ref, src_ref,
    pre_out, sums_out,
    wg, wbuf, grad, act_t, slope, acc, send_a, send_b, out_ref, u_buf, pre_ref,
    f1a, l1a, r1a, f1b, l1b, r1b, f2a, l2a, r2a, f2b, l2b, r2b,
    local_sem, out_sem, w_sem, z_send, z_recv, s_send, s_recv, d_send, d_recv,
):
    dp = lax.axis_index("dp")
    mp = lax.axis_index("mp")
    y, x = dp // 4, lax.rem(dp, 4)
    z, core = mp // 2, lax.rem(mp, 2)

    def step(p, d):
        return lax.rem(p + d + 4, 4)

    z_right, z_left, z_far = step(z, 1), step(z, -1), step(z, 2)
    dev_z = ((dp, z_right * 2 + core), (dp, z_left * 2 + core))
    dev_sib = (dp, z * 2 + 1 - core)
    dev_x = ((y * 4 + step(x, 1), mp), (y * 4 + step(x, -1), mp))
    dev_y = ((step(y, 1) * 4 + x, mp), (step(y, -1) * 4 + x, mp))

    barrier = pltpu.get_barrier_semaphore()
    peers = (*dev_z, dev_sib, *dev_x, *dev_y, (y * 4 + step(x, 2), mp), (step(y, 2) * 4 + x, mp))
    for peer in peers:
        pl.semaphore_signal(barrier, inc=1, device_id=peer, device_id_type=MESH)

    def w_load(zp, slot, sem):
        cols = pl.ds(pl.multiple_of(zp * PAIR, LANES), PAIR)
        return pltpu.make_async_copy(w_ref.at[:, cols], wbuf.at[slot], w_sem.at[sem])

    mine = pl.ds(pl.multiple_of(core * PART, LANES), PART)
    other = pl.ds(pl.multiple_of((1 - core) * PART, LANES), PART)
    own_copy = pltpu.make_async_copy(g_ref, grad.at[z, :, mine], local_sem.at[0])
    u_copy = pltpu.make_async_copy(u_ref, u_buf, local_sem.at[1])
    u_copy.start()
    own_copy.start()
    loads = [w_load(z, 0, 0), w_load(z_left, 1, 1), w_load(z_right, 2, 2), w_load(z_far, 0, 3)]
    pl.semaphore_wait(barrier, len(peers))

    h0, h1 = pl.ds(0, HALF), pl.ds(HALF, HALF)

    def remote(src, dst, s_sem, r_sem, device):
        return pltpu.make_async_remote_copy(
            src_ref=src, dst_ref=dst, send_sem=s_sem, recv_sem=r_sem, device_id=device, device_id_type=MESH
        )

    def z_copy(n, src, zp, rows, way):
        return remote(src, grad.at[zp, rows, mine], z_send.at[n], z_recv.at[n], dev_z[way])

    def piece(zp, rows, col, width):
        return grad.at[zp, rows, pl.ds(pl.multiple_of(core * PART + col, LANES), width)]

    def z_pass(n, zp, rows, col, width, way):
        part = piece(zp, rows, col, width)
        return remote(part, part, z_send.at[n], z_recv.at[n], dev_z[way])

    def s_copy(n, zp, rows, col=0, width=PART):
        part = piece(zp, rows, col, width)
        return remote(part, part, s_send.at[n], s_recv.at[n], dev_sib)

    z_own = [
        z_copy(0, g_ref.at[h0], z, h0, 0),
        z_copy(1, g_ref.at[h1], z, h1, 1),
        z_copy(2, g_ref.at[h1], z, h1, 0),
        z_copy(3, g_ref.at[h0], z, h0, 1),
    ]
    s_own = remote(g_ref, grad.at[z, :, mine], s_send.at[0], s_recv.at[0], dev_sib)
    z_own[0].start()
    z_own[1].start()
    s_own.start()
    z_fwd = [
        z_pass(4, z_left, h0, 0, CUT, 0),
        z_pass(5, z_right, h1, 0, CUT, 1),
        z_pass(6, z_left, h0, CUT, PART - CUT, 0),
        z_pass(7, z_right, h1, CUT, PART - CUT, 1),
    ]
    s_fwd = [
        s_copy(1, z_left, h0),
        s_copy(2, z_right, h1),
        s_copy(3, z_left, h1),
        s_copy(4, z_right, h0),
        s_copy(5, z_far, h0, 0, CUT),
        s_copy(6, z_far, h1, 0, CUT),
        s_copy(7, z_far, h0, CUT, PART - CUT),
        s_copy(8, z_far, h1, CUT, PART - CUT),
    ]

    wg[pl.ds(NBLK, GROUP), :] = jnp.zeros((GROUP, LANES), jnp.float32)

    u_copy.wait()
    for load in loads[:3]:
        load.start()

    def gelu(n, carry):
        tok = pl.ds(pl.multiple_of(lax.rem(n, 4) * LANES, LANES), LANES)
        hid = pl.ds(pl.multiple_of((n // 4) * LANES, LANES), LANES)
        values = u_buf[tok, hid].astype(jnp.float32)
        cdf = 0.5 * (1.0 + lax.erf(values * half_root))
        density = jnp.exp(-0.5 * values * values) * inv_root_tau
        act_t[hid, tok] = (values * cdf).T.astype(jnp.bfloat16)
        slope[tok, hid] = cdf + values * density
        return carry

    lax.fori_loop(0, 4 * (HID // LANES), gelu, 0)

    def weight_grad(zp, n, part_cols, width):
        cols = pl.ds(pl.multiple_of(part_cols + n * width, LANES), width)
        first = zp * (PAIR // LANES) + (part_cols + n * width) // LANES
        for half in range(2):
            product = jnp.dot(
                act_t[pl.ds(half * PART, PART), :], grad[zp, :, cols], preferred_element_type=jnp.float32
            )
            for c in range(width // LANES):
                row = pl.multiple_of((first + c) * HID + half * PART, LANES)
                wg[pl.ds(row, PART), :] = product[:, c * LANES : (c + 1) * LANES]

    def weight_grad_pair(zp):
        def body(n, carry):
            weight_grad(zp, n, 0, 256)
            return carry

        lax.fori_loop(0, PAIR // 256, body, 0)

    def pre_product(zp, slot, rows, mode):
        def body(n, carry):
            hid = pl.ds(pl.multiple_of(n * 256, LANES), 256)
            product = lax.dot_general(
                grad[zp, rows, :], wbuf[slot, hid, :], (((1,), (1,)), ((), ())),
                preferred_element_type=jnp.float32,
            )
            if mode == "first":
                acc[rows, hid] = product
            elif mode == "add":
                acc[rows, hid] += product
            else:
                pre_ref[rows, hid] = ((acc[rows, hid] + product) * slope[rows, hid]).astype(jnp.bfloat16)
            return carry

        lax.fori_loop(0, HID // 256, body, 0)

    whole = pl.ds(0, TOK)
    own_copy.wait()
    s_own.wait_recv()
    weight_grad_pair(z)
    z_own[2].start()
    z_own[3].start()
    loads[0].wait()
    pre_product(z, 0, whole, "first")
    loads[3].start()
    z_own[0].wait_recv()
    s_fwd[0].start()
    z_own[1].wait_recv()
    s_fwd[1].start()
    loads[1].wait()
    loads[2].wait()
    s_fwd[0].wait_recv()
    pre_product(z_left, 1, h0, "add")
    s_fwd[1].wait_recv()
    pre_product(z_right, 2, h1, "add")
    z_fwd[0].start()
    z_fwd[1].start()
    z_own[2].wait_recv()
    s_fwd[2].start()
    z_own[3].wait_recv()
    s_fwd[3].start()
    z_fwd[2].start()
    z_fwd[3].start()
    s_fwd[2].wait_recv()
    weight_grad_pair(z_left)
    z_fwd[0].wait_recv()
    s_fwd[4].start()
    z_fwd[1].wait_recv()
    s_fwd[5].start()
    s_fwd[3].wait_recv()
    weight_grad_pair(z_right)
    weight_grad(z_far, 0, core * PART, CUT)
    for way in range(2):
        s_fwd[4 + way].wait_recv()
    weight_grad(z_far, 0, (1 - core) * PART, CUT)
    for way in range(2):
        z_fwd[2 + way].wait_recv()
        s_fwd[6 + way].start()
    weight_grad(z_far, 0, core * PART + CUT, PART - CUT)
    for way in range(2):
        s_fwd[6 + way].wait_recv()
    weight_grad(z_far, 0, (1 - core) * PART + CUT, PART - CUT)

    scale = 1.0 / math.sqrt(TOK * 16)
    FAR, NEXT, PREV, OWN = range(4)
    SHIFT = (2, 1, -1, 0)
    parts = ((FAR, NEXT), (PREV, OWN))
    send = (send_a, send_b)
    bufs = (
        ((f1a, l1a, r1a), (f2a, l2a, r2a)),
        ((f1b, l1b, r1b), (f2b, l2b, r2b)),
    )

    def axis(half, level):
        along_x = half == level
        places = tuple(step(x if along_x else y, shift) for shift in SHIFT)
        devices = tuple((y * 4 + p, mp) if along_x else (p * 4 + x, mp) for p in places)
        return places, devices

    def gather(half, part, place, row, count):
        low = SPLIT[half][0]
        one = axis(half, 0)[0][place]
        regions = []
        for second in parts[part]:
            two = axis(half, 1)[0][second]
            regions.append((second, (two * 4 + one if half == 0 else one * 4 + two) * SLOTS + low))

        def body(n, carry):
            at = pl.multiple_of(row + n * GROUP, GROUP)
            for second, first in regions:
                taken = [wg[pl.ds(src_ref[0, first + at + s], 1), :] for s in range(GROUP)]
                send[half][second, place, pl.ds(at, GROUP), :] = (
                    jnp.concatenate(taken, axis=0) * scale
                ).astype(jnp.bfloat16)
            return carry

        lax.fori_loop(0, count // GROUP, body, 0)

    def scatter_first(half, part):
        devices = axis(half, 0)[1]
        lead = pl.ds(2 * part, 2)
        base = 32 * half + 3 * part

        def copy(place, dst):
            return remote(
                send[half].at[lead, place], dst.at[lead], d_send.at[base + place], d_recv.at[base + place],
                devices[place],
            )

        far, left, right = bufs[half][0]
        return (copy(FAR, far), copy(NEXT, left), copy(PREV, right))

    def scatter_second(half):
        devices = axis(half, 1)[1]
        far, left, right = bufs[half][1]

        def copy(n, place, dst):
            return remote(
                send[half].at[place, OWN], dst,
                d_send.at[32 * half + 12 + n], d_recv.at[32 * half + 12 + n], devices[place],
            )

        return (copy(0, FAR, far), copy(1, NEXT, left), copy(2, PREV, right))

    def add_first(half, part):
        far, left, right = bufs[half][0]
        for second in parts[part]:
            send[half][second, OWN] = (
                send[half][second, OWN].astype(jnp.float32)
                + far[second].astype(jnp.float32)
                + left[second].astype(jnp.float32)
                + right[second].astype(jnp.float32)
            ).astype(jnp.bfloat16)

    def add_second(half):
        low, a, b = SPLIT[half]
        far, left, right = bufs[half][1]
        out_ref[y, x, pl.ds(low, a + b), :] = (
            send[half][OWN, OWN].astype(jnp.float32)
            + far[...].astype(jnp.float32)
            + left[...].astype(jnp.float32)
            + right[...].astype(jnp.float32)
        ).astype(jnp.bfloat16)

    first = [[scatter_first(half, part) for part in range(2)] for half in range(2)]
    second = [scatter_second(half) for half in range(2)]

    for part in range(2):
        for place in (FAR, NEXT, PREV):
            for half in range(2):
                gather(half, part, place, 0, SPLIT[half][1] + SPLIT[half][2])
                first[half][part][place].start()
    for part in range(2):
        for half in range(2):
            gather(half, part, OWN, 0, SPLIT[half][1] + SPLIT[half][2])
    for part in range(2):
        for half in range(2):
            for copy in first[half][part]:
                copy.wait_recv()
            add_first(half, part)
            for place in parts[part]:
                if place != OWN:
                    second[half][place].start()
        if part == 0:
            pre_product(z_left, 1, h1, "add")
        else:
            pre_product(z_right, 2, h0, "add")

    def spread_copies(half):
        low, a, b = SPLIT[half]
        devices = axis(half, 1)[1]
        part = out_ref.at[y, x, pl.ds(low, a + b)]
        base = 32 * half + 15
        return [
            remote(part, part, d_send.at[base + place], d_recv.at[base + place], devices[place])
            for place in (FAR, NEXT, PREV)
        ]

    def region_copies(half, place):
        low, a, b = SPLIT[half]
        places, devices = axis(half, 0)
        q = axis(half, 1)[0][place]
        base = 32 * half + 18 + 3 * place

        def copy(n, column, row, count, way):
            rows = pl.ds(low + row, count)
            part = out_ref.at[q, column, rows] if half == 0 else out_ref.at[column, q, rows]
            return remote(part, part, d_send.at[base + n], d_recv.at[base + n], devices[way])

        return tuple(copy(n, places[OWN], 0, a + b, way) for n, way in enumerate((NEXT, PREV, FAR)))

    third = [spread_copies(half) for half in range(2)]
    fourth = [[region_copies(half, place) for place in range(4)] for half in range(2)]

    def send_region(half, place):
        for copy in fourth[half][place]:
            copy.start()

    for half in range(2):
        for copy in second[half]:
            copy.wait_recv()
        add_second(half)
        for place in (NEXT, PREV, FAR):
            third[half][place].start()
    for half in range(2):
        send_region(half, OWN)
    loads[3].wait()
    pre_product(z_far, 0, whole, "last")
    pre_copy = pltpu.make_async_copy(pre_ref, pre_out, local_sem.at[2])
    pre_copy.start()
    for place, arrived in ((NEXT, PREV), (PREV, NEXT), (FAR, FAR)):
        for half in range(2):
            third[half][arrived].wait_recv()
            send_region(half, place)
    stores = []
    for place in (OWN, NEXT, PREV, FAR):
        for half in range(2):
            low, a, b = SPLIT[half]
            for copy in fourth[half][place]:
                copy.wait_recv()
            q, rows = axis(half, 1)[0][place], pl.ds(low, a + b)
            at = (q, slice(None), rows) if half == 0 else (slice(None), q, rows)
            stores.append(pltpu.make_async_copy(out_ref.at[at], sums_out.at[at], out_sem.at[4 * half + place]))
            stores[-1].start()
    for store in stores:
        store.wait()
    pre_copy.wait()

    for copy in (*z_own, s_own, *z_fwd, *s_fwd):
        copy.wait_send()
    for half in range(2):
        groups = (*first[half], second[half], third[half], *fourth[half])
        for copy in (c for group in groups for c in group):
            copy.wait_send()


def fused(u, grad_part, weights, source):
    rows_a = SPLIT[0][1] + SPLIT[0][2]
    rows_b = SPLIT[1][1] + SPLIT[1][2]
    big = [pltpu.VMEM((4, rows, LANES), jnp.bfloat16) for rows in (rows_a, rows_b) for _ in range(3)]
    small = [pltpu.VMEM((rows, LANES), jnp.bfloat16) for rows in (rows_a, rows_b) for _ in range(3)]
    vmem = pl.BlockSpec(memory_space=pltpu.VMEM)
    hbm = pl.BlockSpec(memory_space=pl.ANY)
    return pl.pallas_call(
        kernel,
        out_shape=(
            jax.ShapeDtypeStruct((TOK, HID), jnp.bfloat16),
            jax.ShapeDtypeStruct((4, 4, KEEP, LANES), jnp.bfloat16),
        ),
        in_specs=[hbm, hbm, hbm, pl.BlockSpec(memory_space=pltpu.SMEM)],
        out_specs=(hbm, hbm),
        scratch_shapes=[
            pltpu.VMEM((NBLK + GROUP, LANES), jnp.float32),
            pltpu.VMEM((3, HID, PAIR), jnp.bfloat16),
            pltpu.VMEM((4, TOK, PAIR), jnp.bfloat16),
            pltpu.VMEM((HID, TOK), jnp.bfloat16),
            pltpu.VMEM((TOK, HID), jnp.float32),
            pltpu.VMEM((TOK, HID), jnp.float32),
            pltpu.VMEM((4, 4, rows_a, LANES), jnp.bfloat16),
            pltpu.VMEM((4, 4, rows_b, LANES), jnp.bfloat16),
            pltpu.VMEM((4, 4, KEEP, LANES), jnp.bfloat16),
            pltpu.VMEM((TOK, HID), jnp.bfloat16),
            pltpu.VMEM((TOK, HID), jnp.bfloat16),
            *big,
            *small,
            pltpu.SemaphoreType.DMA((3,)),
            pltpu.SemaphoreType.DMA((8,)),
            pltpu.SemaphoreType.DMA((4,)),
            pltpu.SemaphoreType.DMA((8,)),
            pltpu.SemaphoreType.DMA((8,)),
            pltpu.SemaphoreType.DMA((9,)),
            pltpu.SemaphoreType.DMA((9,)),
            pltpu.SemaphoreType.DMA((64,)),
            pltpu.SemaphoreType.DMA((64,)),
        ],
        compiler_params=pltpu.CompilerParams(
            collective_id=0, has_side_effects=True, vmem_limit_bytes=57 * 1024 * 1024
        ),
        cost_estimate=pl.CostEstimate(
            flops=4 * TOK * HID * WIDTH, bytes_accessed=20_000_000, transcendentals=2 * TOK * HID
        ),
    )(u, grad_part, weights, source)


FINISH = 4


def finish_kernel(pre_ref, sums_ref, pre_out, sums_out, pre_buf, sums_buf, wide_buf, in_sem, out_sem):
    slots = 16 * KEEP // FINISH
    pre_in = pltpu.make_async_copy(pre_ref, pre_buf, in_sem.at[FINISH])
    pre_back = pltpu.make_async_copy(pre_buf, pre_out, out_sem.at[FINISH])
    parts = [pl.ds(n * slots, slots) for n in range(FINISH)]
    loads = [pltpu.make_async_copy(sums_ref.at[part], sums_buf.at[part], in_sem.at[n]) for n, part in enumerate(parts)]
    stores = [pltpu.make_async_copy(wide_buf.at[part], sums_out.at[part], out_sem.at[n]) for n, part in enumerate(parts)]
    pre_in.start()
    for load in loads:
        load.start()
    pre_in.wait()
    pre_back.start()
    for part, load, store in zip(parts, loads, stores):
        load.wait()
        wide_buf[part, :] = sums_buf[part, :].astype(jnp.float32)
        store.start()
    for store in stores:
        store.wait()
    pre_back.wait()


def finish(pre_grad, sums):
    hbm = pl.BlockSpec(memory_space=pltpu.HBM)
    return pl.pallas_call(
        finish_kernel,
        out_shape=(
            jax.ShapeDtypeStruct((TOK, HID), jnp.bfloat16),
            jax.ShapeDtypeStruct((16 * KEEP, LANES), jnp.float32),
        ),
        in_specs=[hbm, hbm],
        out_specs=(hbm, hbm),
        scratch_shapes=[
            pltpu.VMEM((TOK, HID), jnp.bfloat16),
            pltpu.VMEM((16 * KEEP, LANES), jnp.bfloat16),
            pltpu.VMEM((16 * KEEP, LANES), jnp.float32),
            pltpu.SemaphoreType.DMA((FINISH + 1,)),
            pltpu.SemaphoreType.DMA((FINISH + 1,)),
        ],
    )(pre_grad, sums)


def local(
    inner_before_nonlinear,
    layer_exit_derivative,
    contract_weights,
    copy_tile_indicator,
    span_opening_tile,
    remaining_tile_flags,
):
    source = slot_sources(
        remaining_tile_flags.reshape(ROWS, LANES), copy_tile_indicator.reshape(ROWS, LANES), span_opening_tile
    )
    pre_grad, sums = fused(inner_before_nonlinear, layer_exit_derivative, contract_weights, source)
    pre_grad, sums = finish(pre_grad, sums.reshape(16 * KEEP, LANES))
    return (pre_grad, sums[None])


def solution(mesh):
    in_specs = (
        P("dp", "mp"),
        P("dp", "mp"),
        P("mp", None),
        P("dp", "mp", None),
        P(),
        P("mp", None),
    )
    out_specs = (P("dp", "mp"), P("mp", None, None))
    return jax.shard_map(local, mesh=mesh, in_specs=in_specs, out_specs=out_specs, check_vma=False)
```

```python
import functools
import math

import jax
import jax.numpy as jnp
from jax import lax
from jax.experimental import pallas as pl
from jax.experimental.pallas import tpu as pltpu
from jax.sharding import PartitionSpec as P

half_root = 0.7071067811865476
inv_root_tau = 0.3989422804014327
MESH = pl.DeviceIdType.MESH

TOK = 512
HID = 1280
WIDTH = 5120
PART = 640
PAIR = 2 * PART
LANES = 128
COLS = WIDTH // LANES
NBLK = HID * COLS
KEEP = 400
HALF = TOK // 2
GROUP = 16
ROWS = NBLK // LANES
ROWS_PAD = 448
WINDOW = 48
SLOTS = 512
CUT = 256
SPLIT = ((0, 112, 96), (208, 96, 96))


def index_kernel(flag_ref, copied_ref, start_ref, src_ref, flags, within, upto, before, opening):
    flags[pl.ds(0, ROWS), :] = flag_ref[...]
    pad = pl.ds(ROWS, ROWS_PAD - ROWS)
    flags[pad, :] = jnp.zeros((ROWS_PAD - ROWS, LANES), jnp.int32)

    def iota(shape, dim):
        return lax.broadcasted_iota(jnp.int32, shape, dim)

    square = (LANES, LANES)
    flag_bf = flags[...].astype(jnp.float32).astype(jnp.bfloat16)
    tri = jnp.where(iota(square, 0) <= iota(square, 1), 1.0, 0.0).astype(jnp.bfloat16)
    within[...] = jnp.dot(flag_bf, tri, preferred_element_type=jnp.float32) - 64.0
    both = (flag_ref[...] * copied_ref[...]).astype(jnp.float32)
    within[pl.ds(0, ROWS), :] = within[pl.ds(0, ROWS), :] + 0.5 * both
    totals = jnp.dot(flag_bf, jnp.ones(square, jnp.bfloat16), preferred_element_type=jnp.float32)
    tall = (ROWS_PAD, ROWS_PAD)
    tri = jnp.where(iota(tall, 0) >= iota(tall, 1), 1.0, 0.0).astype(jnp.bfloat16)
    sums = jnp.dot(tri, totals.astype(jnp.bfloat16), preferred_element_type=jnp.float32)
    upto[...] = sums
    before[...] = sums - totals
    for o in range(17):
        start = start_ref[o]
        row = pl.ds(lax.shift_right_logical(start, 7), 1)
        inside = jnp.where(iota((1, LANES), 1) < lax.bitwise_and(start, 127), flags[row, :], 0).astype(jnp.float32)
        opening[pl.ds(o, 1), :] = before[row, :] + jnp.sum(inside, axis=1, keepdims=True)

    def wide(v):
        return jnp.concatenate([v] * (SLOTS // LANES), axis=1)

    def sources(o):
        row0 = pl.multiple_of(lax.bitwise_and(lax.shift_right_logical(start_ref[o], 7), -8), 8)
        rows = pl.ds(row0, WINDOW)
        target = wide(opening[pl.ds(o, 1), :]) + iota((1, SLOTS), 1).astype(jnp.float32)
        limit = wide(opening[pl.ds(o + 1, 1), :])
        ends = wide(upto[rows, :])
        passed = ends <= target
        count = jnp.sum(jnp.where(passed, 1.0, 0.0), axis=0, keepdims=True)
        last = jnp.max(jnp.where(passed, ends, wide(before[pl.ds(row0, 1), :])), axis=0, keepdims=True)
        pick = jnp.where(iota((WINDOW, SLOTS), 0).astype(jnp.float32) == count, 1.0, 0.0).astype(jnp.bfloat16)

        found = lax.dot_general(
            within[rows, :].astype(jnp.bfloat16), pick, (((0,), (0,)), ((), ())), preferred_element_type=jnp.float32
        )
        rest = target - last - 64.0
        at = jnp.sum(jnp.where(found < rest + 0.75, 1.0, 0.0), axis=0, keepdims=True)
        kept = jnp.sum(jnp.where(found == rest + 1.5, 1.0, 0.0), axis=0, keepdims=True)
        block = (count + row0.astype(jnp.float32)) * LANES + at
        hid = jnp.floor((block + 0.5) * (1.0 / COLS))
        source = (block - hid * COLS) * HID + hid
        source = jnp.where((target < limit) & (kept > 0.5), source, float(NBLK))
        src_ref[:, pl.ds(o * SLOTS, SLOTS)] = source.astype(jnp.int32)

    for o in range(16):
        sources(o)


def slot_sources(flags, copied, starts):
    vmem = pl.BlockSpec(memory_space=pltpu.VMEM)
    table = pltpu.VMEM((ROWS_PAD, LANES), jnp.float32)
    return pl.pallas_call(
        index_kernel,
        out_shape=jax.ShapeDtypeStruct((1, 16 * SLOTS), jnp.int32),
        in_specs=[vmem, vmem, pl.BlockSpec(memory_space=pltpu.SMEM)],
        out_specs=vmem,
        scratch_shapes=[
            pltpu.VMEM((ROWS_PAD, LANES), jnp.int32),
            table,
            table,
            table,
            pltpu.VMEM((24, LANES), jnp.float32),
        ],
    )(flags, copied, starts)


def kernel(
    u_ref, g_ref, w_ref, src_ref,
    pre_out, sums_out,
    wg, wbuf, grad, act_t, slope, acc, send_a, send_b, out_ref, u_buf, pre_ref,
    f1a, l1a, r1a, f1b, l1b, r1b, f2a, l2a, r2a, f2b, l2b, r2b,
    local_sem, out_sem, w_sem, z_send, z_recv, s_send, s_recv, d_send, d_recv,
):
    dp = lax.axis_index("dp")
    mp = lax.axis_index("mp")
    y, x = dp // 4, lax.rem(dp, 4)
    z, core = mp // 2, lax.rem(mp, 2)

    def step(p, d):
        return lax.rem(p + d + 4, 4)

    z_right, z_left, z_far = step(z, 1), step(z, -1), step(z, 2)
    dev_z = ((dp, z_right * 2 + core), (dp, z_left * 2 + core))
    dev_sib = (dp, z * 2 + 1 - core)
    dev_x = ((y * 4 + step(x, 1), mp), (y * 4 + step(x, -1), mp))
    dev_y = ((step(y, 1) * 4 + x, mp), (step(y, -1) * 4 + x, mp))

    barrier = pltpu.get_barrier_semaphore()
    peers = (*dev_z, dev_sib, *dev_x, *dev_y, (y * 4 + step(x, 2), mp), (step(y, 2) * 4 + x, mp))
    for peer in peers:
        pl.semaphore_signal(barrier, inc=1, device_id=peer, device_id_type=MESH)

    def w_load(zp, slot, sem):
        cols = pl.ds(pl.multiple_of(zp * PAIR, LANES), PAIR)
        return pltpu.make_async_copy(w_ref.at[:, cols], wbuf.at[slot], w_sem.at[sem])

    mine = pl.ds(pl.multiple_of(core * PART, LANES), PART)
    other = pl.ds(pl.multiple_of((1 - core) * PART, LANES), PART)
    own_copy = pltpu.make_async_copy(g_ref, grad.at[z, :, mine], local_sem.at[0])
    u_copy = pltpu.make_async_copy(u_ref, u_buf, local_sem.at[1])
    u_copy.start()
    own_copy.start()
    loads = [w_load(z, 0, 0), w_load(z_left, 1, 1), w_load(z_right, 2, 2), w_load(z_far, 0, 3)]
    pl.semaphore_wait(barrier, len(peers))

    h0, h1 = pl.ds(0, HALF), pl.ds(HALF, HALF)

    def remote(src, dst, s_sem, r_sem, device):
        return pltpu.make_async_remote_copy(
            src_ref=src, dst_ref=dst, send_sem=s_sem, recv_sem=r_sem, device_id=device, device_id_type=MESH
        )

    def z_copy(n, src, zp, rows, way):
        return remote(src, grad.at[zp, rows, mine], z_send.at[n], z_recv.at[n], dev_z[way])

    def piece(zp, rows, col, width):
        return grad.at[zp, rows, pl.ds(pl.multiple_of(core * PART + col, LANES), width)]

    def z_pass(n, zp, rows, col, width, way):
        part = piece(zp, rows, col, width)
        return remote(part, part, z_send.at[n], z_recv.at[n], dev_z[way])

    def s_copy(n, zp, rows, col=0, width=PART):
        part = piece(zp, rows, col, width)
        return remote(part, part, s_send.at[n], s_recv.at[n], dev_sib)

    z_own = [
        z_copy(0, g_ref.at[h0], z, h0, 0),
        z_copy(1, g_ref.at[h1], z, h1, 1),
        z_copy(2, g_ref.at[h1], z, h1, 0),
        z_copy(3, g_ref.at[h0], z, h0, 1),
    ]
    s_own = remote(g_ref, grad.at[z, :, mine], s_send.at[0], s_recv.at[0], dev_sib)
    z_own[0].start()
    z_own[1].start()
    s_own.start()
    z_fwd = [
        z_pass(4, z_left, h0, 0, CUT, 0),
        z_pass(5, z_right, h1, 0, CUT, 1),
        z_pass(6, z_left, h0, CUT, PART - CUT, 0),
        z_pass(7, z_right, h1, CUT, PART - CUT, 1),
    ]
    s_fwd = [
        s_copy(1, z_left, h0),
        s_copy(2, z_right, h1),
        s_copy(3, z_left, h1),
        s_copy(4, z_right, h0),
        s_copy(5, z_far, h0, 0, CUT),
        s_copy(6, z_far, h1, 0, CUT),
        s_copy(7, z_far, h0, CUT, PART - CUT),
        s_copy(8, z_far, h1, CUT, PART - CUT),
    ]

    wg[pl.ds(NBLK, GROUP), :] = jnp.zeros((GROUP, LANES), jnp.float32)

    u_copy.wait()
    for load in loads[:3]:
        load.start()

    def gelu(n, carry):
        tok = pl.ds(pl.multiple_of(lax.rem(n, 4) * LANES, LANES), LANES)
        hid = pl.ds(pl.multiple_of((n // 4) * LANES, LANES), LANES)
        values = u_buf[tok, hid].astype(jnp.float32)
        cdf = 0.5 * (1.0 + lax.erf(values * half_root))
        density = jnp.exp(-0.5 * values * values) * inv_root_tau
        act_t[hid, tok] = (values * cdf).T.astype(jnp.bfloat16)
        slope[tok, hid] = cdf + values * density
        return carry

    lax.fori_loop(0, 4 * (HID // LANES), gelu, 0)

    def weight_grad(zp, n, part_cols, width):
        cols = pl.ds(pl.multiple_of(part_cols + n * width, LANES), width)
        first = zp * (PAIR // LANES) + (part_cols + n * width) // LANES
        for half in range(2):
            product = jnp.dot(
                act_t[pl.ds(half * PART, PART), :], grad[zp, :, cols], preferred_element_type=jnp.float32
            )
            for c in range(width // LANES):
                row = pl.multiple_of((first + c) * HID + half * PART, LANES)
                wg[pl.ds(row, PART), :] = product[:, c * LANES : (c + 1) * LANES]

    def weight_grad_pair(zp):
        def body(n, carry):
            weight_grad(zp, n, 0, 256)
            return carry

        lax.fori_loop(0, PAIR // 256, body, 0)

    def pre_product(zp, slot, rows, mode):
        def body(n, carry):
            hid = pl.ds(pl.multiple_of(n * 256, LANES), 256)
            product = lax.dot_general(
                grad[zp, rows, :], wbuf[slot, hid, :], (((1,), (1,)), ((), ())),
                preferred_element_type=jnp.float32,
            )
            if mode == "first":
                acc[rows, hid] = product
            elif mode == "add":
                acc[rows, hid] += product
            else:
                pre_ref[rows, hid] = ((acc[rows, hid] + product) * slope[rows, hid]).astype(jnp.bfloat16)
            return carry

        lax.fori_loop(0, HID // 256, body, 0)

    whole = pl.ds(0, TOK)
    own_copy.wait()
    s_own.wait_recv()
    weight_grad_pair(z)
    z_own[2].start()
    z_own[3].start()
    loads[0].wait()
    pre_product(z, 0, whole, "first")
    loads[3].start()
    z_own[0].wait_recv()
    s_fwd[0].start()
    z_own[1].wait_recv()
    s_fwd[1].start()
    loads[1].wait()
    loads[2].wait()
    s_fwd[0].wait_recv()
    pre_product(z_left, 1, h0, "add")
    s_fwd[1].wait_recv()
    pre_product(z_right, 2, h1, "add")
    z_fwd[0].start()
    z_fwd[1].start()
    z_own[2].wait_recv()
    s_fwd[2].start()
    z_own[3].wait_recv()
    s_fwd[3].start()
    z_fwd[2].start()
    z_fwd[3].start()
    s_fwd[2].wait_recv()
    weight_grad_pair(z_left)
    z_fwd[0].wait_recv()
    s_fwd[4].start()
    z_fwd[1].wait_recv()
    s_fwd[5].start()
    s_fwd[3].wait_recv()
    weight_grad_pair(z_right)
    weight_grad(z_far, 0, core * PART, CUT)
    for way in range(2):
        s_fwd[4 + way].wait_recv()
    weight_grad(z_far, 0, (1 - core) * PART, CUT)
    for way in range(2):
        z_fwd[2 + way].wait_recv()
        s_fwd[6 + way].start()
    weight_grad(z_far, 0, core * PART + CUT, PART - CUT)
    for way in range(2):
        s_fwd[6 + way].wait_recv()
    weight_grad(z_far, 0, (1 - core) * PART + CUT, PART - CUT)

    scale = 1.0 / math.sqrt(TOK * 16)
    FAR, NEXT, PREV, OWN = range(4)
    SHIFT = (2, 1, -1, 0)
    parts = ((FAR,), (NEXT, PREV), (OWN,))
    send = (send_a, send_b)
    bufs = (
        ((f1a, l1a, r1a), (f2a, l2a, r2a)),
        ((f1b, l1b, r1b), (f2b, l2b, r2b)),
    )

    def axis(half, level):
        along_x = half == level
        places = tuple(step(x if along_x else y, shift) for shift in SHIFT)
        devices = tuple((y * 4 + p, mp) if along_x else (p * 4 + x, mp) for p in places)
        return places, devices

    def gather(half, part, place, row, count):
        low = SPLIT[half][0]
        one = axis(half, 0)[0][place]
        regions = []
        for second in parts[part]:
            two = axis(half, 1)[0][second]
            regions.append((second, (two * 4 + one if half == 0 else one * 4 + two) * SLOTS + low))

        def body(n, carry):
            at = pl.multiple_of(row + n * GROUP, GROUP)
            for second, first in regions:
                taken = [wg[pl.ds(src_ref[0, first + at + s], 1), :] for s in range(GROUP)]
                send[half][second, place, pl.ds(at, GROUP), :] = (
                    jnp.concatenate(taken, axis=0) * scale
                ).astype(jnp.bfloat16)
            return carry

        lax.fori_loop(0, count // GROUP, body, 0)

    def scatter_first(half, part):
        devices = axis(half, 0)[1]
        lead = pl.ds(parts[part][0], len(parts[part]))
        base = 32 * half + 3 * part

        def copy(place, dst):
            return remote(
                send[half].at[lead, place], dst.at[lead], d_send.at[base + place], d_recv.at[base + place],
                devices[place],
            )

        far, left, right = bufs[half][0]
        return (copy(FAR, far), copy(NEXT, left), copy(PREV, right))

    def scatter_second(half):
        devices = axis(half, 1)[1]
        far, left, right = bufs[half][1]

        def copy(n, place, dst):
            return remote(
                send[half].at[place, OWN], dst,
                d_send.at[32 * half + 12 + n], d_recv.at[32 * half + 12 + n], devices[place],
            )

        return (copy(0, FAR, far), copy(1, NEXT, left), copy(2, PREV, right))

    def add_first(half, part):
        far, left, right = bufs[half][0]
        for second in parts[part]:
            send[half][second, OWN] = (
                send[half][second, OWN].astype(jnp.float32)
                + far[second].astype(jnp.float32)
                + left[second].astype(jnp.float32)
                + right[second].astype(jnp.float32)
            ).astype(jnp.bfloat16)

    def add_second(half):
        low, a, b = SPLIT[half]
        far, left, right = bufs[half][1]
        out_ref[y, x, pl.ds(low, a + b), :] = (
            send[half][OWN, OWN].astype(jnp.float32)
            + far[...].astype(jnp.float32)
            + left[...].astype(jnp.float32)
            + right[...].astype(jnp.float32)
        ).astype(jnp.bfloat16)

    first = [[scatter_first(half, part) for part in range(3)] for half in range(2)]
    second = [scatter_second(half) for half in range(2)]

    for part in range(3):
        for place in (FAR, NEXT, PREV):
            for half in range(2):
                gather(half, part, place, 0, SPLIT[half][1] + SPLIT[half][2])
                first[half][part][place].start()
    for part in range(3):
        for half in range(2):
            gather(half, part, OWN, 0, SPLIT[half][1] + SPLIT[half][2])
    for part in range(3):
        for half in range(2):
            for copy in first[half][part]:
                copy.wait_recv()
            add_first(half, part)
            for place in parts[part]:
                if place != OWN:
                    second[half][place].start()
        if part == 0:
            pre_product(z_left, 1, h1, "add")
        elif part == 1:
            pre_product(z_right, 2, h0, "add")

    def spread_copies(half):
        low, a, b = SPLIT[half]
        devices = axis(half, 1)[1]
        part = out_ref.at[y, x, pl.ds(low, a + b)]
        base = 32 * half + 15
        return [
            remote(part, part, d_send.at[base + place], d_recv.at[base + place], devices[place])
            for place in (FAR, NEXT, PREV)
        ]

    def region_copies(half, place):
        low, a, b = SPLIT[half]
        places, devices = axis(half, 0)
        q = axis(half, 1)[0][place]
        base = 32 * half + 18 + 3 * place

        def copy(n, column, row, count, way):
            rows = pl.ds(low + row, count)
            part = out_ref.at[q, column, rows] if half == 0 else out_ref.at[column, q, rows]
            return remote(part, part, d_send.at[base + n], d_recv.at[base + n], devices[way])

        return tuple(copy(n, places[OWN], 0, a + b, way) for n, way in enumerate((NEXT, PREV, FAR)))

    third = [spread_copies(half) for half in range(2)]
    fourth = [[region_copies(half, place) for place in range(4)] for half in range(2)]

    def send_region(half, place):
        for copy in fourth[half][place]:
            copy.start()

    for half in range(2):
        for copy in second[half]:
            copy.wait_recv()
        add_second(half)
        for place in (NEXT, PREV, FAR):
            third[half][place].start()
    for half in range(2):
        send_region(half, OWN)
    loads[3].wait()
    pre_product(z_far, 0, whole, "last")
    pre_copy = pltpu.make_async_copy(pre_ref, pre_out, local_sem.at[2])
    pre_copy.start()
    for place, arrived in ((NEXT, PREV), (PREV, NEXT), (FAR, FAR)):
        for half in range(2):
            third[half][arrived].wait_recv()
            send_region(half, place)
    stores = []
    for place in (OWN, NEXT, PREV, FAR):
        for half in range(2):
            low, a, b = SPLIT[half]
            for copy in fourth[half][place]:
                copy.wait_recv()
            q, rows = axis(half, 1)[0][place], pl.ds(low, a + b)
            at = (q, slice(None), rows) if half == 0 else (slice(None), q, rows)
            stores.append(pltpu.make_async_copy(out_ref.at[at], sums_out.at[at], out_sem.at[4 * half + place]))
            stores[-1].start()
    for store in stores:
        store.wait()
    pre_copy.wait()

    for copy in (*z_own, s_own, *z_fwd, *s_fwd):
        copy.wait_send()
    for half in range(2):
        groups = (*first[half], second[half], third[half], *fourth[half])
        for copy in (c for group in groups for c in group):
            copy.wait_send()


def fused(u, grad_part, weights, source):
    rows_a = SPLIT[0][1] + SPLIT[0][2]
    rows_b = SPLIT[1][1] + SPLIT[1][2]
    big = [pltpu.VMEM((4, rows, LANES), jnp.bfloat16) for rows in (rows_a, rows_b) for _ in range(3)]
    small = [pltpu.VMEM((rows, LANES), jnp.bfloat16) for rows in (rows_a, rows_b) for _ in range(3)]
    vmem = pl.BlockSpec(memory_space=pltpu.VMEM)
    hbm = pl.BlockSpec(memory_space=pl.ANY)
    return pl.pallas_call(
        kernel,
        out_shape=(
            jax.ShapeDtypeStruct((TOK, HID), jnp.bfloat16),
            jax.ShapeDtypeStruct((4, 4, KEEP, LANES), jnp.bfloat16),
        ),
        in_specs=[hbm, hbm, hbm, pl.BlockSpec(memory_space=pltpu.SMEM)],
        out_specs=(hbm, hbm),
        scratch_shapes=[
            pltpu.VMEM((NBLK + GROUP, LANES), jnp.float32),
            pltpu.VMEM((3, HID, PAIR), jnp.bfloat16),
            pltpu.VMEM((4, TOK, PAIR), jnp.bfloat16),
            pltpu.VMEM((HID, TOK), jnp.bfloat16),
            pltpu.VMEM((TOK, HID), jnp.float32),
            pltpu.VMEM((TOK, HID), jnp.float32),
            pltpu.VMEM((4, 4, rows_a, LANES), jnp.bfloat16),
            pltpu.VMEM((4, 4, rows_b, LANES), jnp.bfloat16),
            pltpu.VMEM((4, 4, KEEP, LANES), jnp.bfloat16),
            pltpu.VMEM((TOK, HID), jnp.bfloat16),
            pltpu.VMEM((TOK, HID), jnp.bfloat16),
            *big,
            *small,
            pltpu.SemaphoreType.DMA((3,)),
            pltpu.SemaphoreType.DMA((8,)),
            pltpu.SemaphoreType.DMA((4,)),
            pltpu.SemaphoreType.DMA((8,)),
            pltpu.SemaphoreType.DMA((8,)),
            pltpu.SemaphoreType.DMA((9,)),
            pltpu.SemaphoreType.DMA((9,)),
            pltpu.SemaphoreType.DMA((64,)),
            pltpu.SemaphoreType.DMA((64,)),
        ],
        compiler_params=pltpu.CompilerParams(
            collective_id=0, has_side_effects=True, vmem_limit_bytes=57 * 1024 * 1024
        ),
        cost_estimate=pl.CostEstimate(
            flops=4 * TOK * HID * WIDTH, bytes_accessed=20_000_000, transcendentals=2 * TOK * HID
        ),
    )(u, grad_part, weights, source)


FINISH = 4


def finish_kernel(pre_ref, sums_ref, pre_out, sums_out, pre_buf, sums_buf, wide_buf, in_sem, out_sem):
    slots = 16 * KEEP // FINISH
    pre_in = pltpu.make_async_copy(pre_ref, pre_buf, in_sem.at[FINISH])
    pre_back = pltpu.make_async_copy(pre_buf, pre_out, out_sem.at[FINISH])
    parts = [pl.ds(n * slots, slots) for n in range(FINISH)]
    loads = [pltpu.make_async_copy(sums_ref.at[part], sums_buf.at[part], in_sem.at[n]) for n, part in enumerate(parts)]
    stores = [pltpu.make_async_copy(wide_buf.at[part], sums_out.at[part], out_sem.at[n]) for n, part in enumerate(parts)]
    for load in loads:
        load.start()
    pre_in.start()
    for part, load, store in zip(parts, loads, stores):
        load.wait()
        wide_buf[part, :] = sums_buf[part, :].astype(jnp.float32)
        store.start()
    pre_in.wait()
    pre_back.start()
    for store in stores:
        store.wait()
    pre_back.wait()


def finish(pre_grad, sums):
    hbm = pl.BlockSpec(memory_space=pltpu.HBM)
    return pl.pallas_call(
        finish_kernel,
        out_shape=(
            jax.ShapeDtypeStruct((TOK, HID), jnp.bfloat16),
            jax.ShapeDtypeStruct((16 * KEEP, LANES), jnp.float32),
        ),
        in_specs=[hbm, hbm],
        out_specs=(hbm, hbm),
        scratch_shapes=[
            pltpu.VMEM((TOK, HID), jnp.bfloat16),
            pltpu.VMEM((16 * KEEP, LANES), jnp.bfloat16),
            pltpu.VMEM((16 * KEEP, LANES), jnp.float32),
            pltpu.SemaphoreType.DMA((FINISH + 1,)),
            pltpu.SemaphoreType.DMA((FINISH + 1,)),
        ],
    )(pre_grad, sums)


def local(
    inner_before_nonlinear,
    layer_exit_derivative,
    contract_weights,
    copy_tile_indicator,
    span_opening_tile,
    remaining_tile_flags,
):
    source = slot_sources(
        remaining_tile_flags.reshape(ROWS, LANES), copy_tile_indicator.reshape(ROWS, LANES), span_opening_tile
    )
    pre_grad, sums = fused(inner_before_nonlinear, layer_exit_derivative, contract_weights, source)
    pre_grad, sums = finish(pre_grad, sums.reshape(16 * KEEP, LANES))
    return (pre_grad, sums[None])


def solution(mesh):
    in_specs = (
        P("dp", "mp"),
        P("dp", "mp"),
        P("mp", None),
        P("dp", "mp", None),
        P(),
        P("mp", None),
    )
    out_specs = (P("dp", "mp"), P("mp", None, None))
    return jax.shard_map(local, mesh=mesh, in_specs=in_specs, out_specs=out_specs, check_vma=False)
```

```python
import functools
import math

import jax
import jax.numpy as jnp
from jax import lax
from jax.experimental import pallas as pl
from jax.experimental.pallas import tpu as pltpu
from jax.sharding import PartitionSpec as P

half_root = 0.7071067811865476
inv_root_tau = 0.3989422804014327
MESH = pl.DeviceIdType.MESH

TOK = 512
HID = 1280
WIDTH = 5120
PART = 640
PAIR = 2 * PART
LANES = 128
COLS = WIDTH // LANES
NBLK = HID * COLS
KEEP = 400
HALF = TOK // 2
GROUP = 16
ROWS = NBLK // LANES
ROWS_PAD = 448
WINDOW = 48
SLOTS = 512
CUT = 128
SPLIT = ((0, 112, 96), (208, 96, 96))


def index_kernel(flag_ref, copied_ref, start_ref, src_ref, flags, within, upto, before, opening):
    flags[pl.ds(0, ROWS), :] = flag_ref[...]
    pad = pl.ds(ROWS, ROWS_PAD - ROWS)
    flags[pad, :] = jnp.zeros((ROWS_PAD - ROWS, LANES), jnp.int32)

    def iota(shape, dim):
        return lax.broadcasted_iota(jnp.int32, shape, dim)

    square = (LANES, LANES)
    flag_bf = flags[...].astype(jnp.float32).astype(jnp.bfloat16)
    tri = jnp.where(iota(square, 0) <= iota(square, 1), 1.0, 0.0).astype(jnp.bfloat16)
    within[...] = jnp.dot(flag_bf, tri, preferred_element_type=jnp.float32) - 64.0
    both = (flag_ref[...] * copied_ref[...]).astype(jnp.float32)
    within[pl.ds(0, ROWS), :] = within[pl.ds(0, ROWS), :] + 0.5 * both
    totals = jnp.dot(flag_bf, jnp.ones(square, jnp.bfloat16), preferred_element_type=jnp.float32)
    tall = (ROWS_PAD, ROWS_PAD)
    tri = jnp.where(iota(tall, 0) >= iota(tall, 1), 1.0, 0.0).astype(jnp.bfloat16)
    sums = jnp.dot(tri, totals.astype(jnp.bfloat16), preferred_element_type=jnp.float32)
    upto[...] = sums
    before[...] = sums - totals
    for o in range(17):
        start = start_ref[o]
        row = pl.ds(lax.shift_right_logical(start, 7), 1)
        inside = jnp.where(iota((1, LANES), 1) < lax.bitwise_and(start, 127), flags[row, :], 0).astype(jnp.float32)
        opening[pl.ds(o, 1), :] = before[row, :] + jnp.sum(inside, axis=1, keepdims=True)

    def wide(v):
        return jnp.concatenate([v] * (SLOTS // LANES), axis=1)

    def sources(o):
        row0 = pl.multiple_of(lax.bitwise_and(lax.shift_right_logical(start_ref[o], 7), -8), 8)
        rows = pl.ds(row0, WINDOW)
        target = wide(opening[pl.ds(o, 1), :]) + iota((1, SLOTS), 1).astype(jnp.float32)
        limit = wide(opening[pl.ds(o + 1, 1), :])
        ends = wide(upto[rows, :])
        passed = ends <= target
        count = jnp.sum(jnp.where(passed, 1.0, 0.0), axis=0, keepdims=True)
        last = jnp.max(jnp.where(passed, ends, wide(before[pl.ds(row0, 1), :])), axis=0, keepdims=True)
        pick = jnp.where(iota((WINDOW, SLOTS), 0).astype(jnp.float32) == count, 1.0, 0.0).astype(jnp.bfloat16)

        found = lax.dot_general(
            within[rows, :].astype(jnp.bfloat16), pick, (((0,), (0,)), ((), ())), preferred_element_type=jnp.float32
        )
        rest = target - last - 64.0
        at = jnp.sum(jnp.where(found < rest + 0.75, 1.0, 0.0), axis=0, keepdims=True)
        kept = jnp.sum(jnp.where(found == rest + 1.5, 1.0, 0.0), axis=0, keepdims=True)
        block = (count + row0.astype(jnp.float32)) * LANES + at
        hid = jnp.floor((block + 0.5) * (1.0 / COLS))
        source = (block - hid * COLS) * HID + hid
        source = jnp.where((target < limit) & (kept > 0.5), source, float(NBLK))
        src_ref[:, pl.ds(o * SLOTS, SLOTS)] = source.astype(jnp.int32)

    for o in range(16):
        sources(o)


def slot_sources(flags, copied, starts):
    vmem = pl.BlockSpec(memory_space=pltpu.VMEM)
    table = pltpu.VMEM((ROWS_PAD, LANES), jnp.float32)
    return pl.pallas_call(
        index_kernel,
        out_shape=jax.ShapeDtypeStruct((1, 16 * SLOTS), jnp.int32),
        in_specs=[vmem, vmem, pl.BlockSpec(memory_space=pltpu.SMEM)],
        out_specs=vmem,
        scratch_shapes=[
            pltpu.VMEM((ROWS_PAD, LANES), jnp.int32),
            table,
            table,
            table,
            pltpu.VMEM((24, LANES), jnp.float32),
        ],
    )(flags, copied, starts)


def kernel(
    u_ref, g_ref, w_ref, src_ref,
    pre_out, sums_out,
    wg, wbuf, grad, act_t, slope, acc, send_a, send_b, out_ref, u_buf, pre_ref,
    f1a, l1a, r1a, f1b, l1b, r1b, f2a, l2a, r2a, f2b, l2b, r2b,
    local_sem, out_sem, w_sem, z_send, z_recv, s_send, s_recv, d_send, d_recv,
):
    dp = lax.axis_index("dp")
    mp = lax.axis_index("mp")
    y, x = dp // 4, lax.rem(dp, 4)
    z, core = mp // 2, lax.rem(mp, 2)

    def step(p, d):
        return lax.rem(p + d + 4, 4)

    z_right, z_left, z_far = step(z, 1), step(z, -1), step(z, 2)
    dev_z = ((dp, z_right * 2 + core), (dp, z_left * 2 + core))
    dev_sib = (dp, z * 2 + 1 - core)
    dev_x = ((y * 4 + step(x, 1), mp), (y * 4 + step(x, -1), mp))
    dev_y = ((step(y, 1) * 4 + x, mp), (step(y, -1) * 4 + x, mp))

    barrier = pltpu.get_barrier_semaphore()
    peers = (*dev_z, dev_sib, *dev_x, *dev_y, (y * 4 + step(x, 2), mp), (step(y, 2) * 4 + x, mp))
    for peer in peers:
        pl.semaphore_signal(barrier, inc=1, device_id=peer, device_id_type=MESH)

    def w_load(zp, slot, sem):
        cols = pl.ds(pl.multiple_of(zp * PAIR, LANES), PAIR)
        return pltpu.make_async_copy(w_ref.at[:, cols], wbuf.at[slot], w_sem.at[sem])

    mine = pl.ds(pl.multiple_of(core * PART, LANES), PART)
    other = pl.ds(pl.multiple_of((1 - core) * PART, LANES), PART)
    own_copy = pltpu.make_async_copy(g_ref, grad.at[z, :, mine], local_sem.at[0])
    u_copy = pltpu.make_async_copy(u_ref, u_buf, local_sem.at[1])
    u_copy.start()
    own_copy.start()
    loads = [w_load(z, 0, 0), w_load(z_left, 1, 1), w_load(z_right, 2, 2), w_load(z_far, 0, 3)]
    pl.semaphore_wait(barrier, len(peers))

    h0, h1 = pl.ds(0, HALF), pl.ds(HALF, HALF)

    def remote(src, dst, s_sem, r_sem, device):
        return pltpu.make_async_remote_copy(
            src_ref=src, dst_ref=dst, send_sem=s_sem, recv_sem=r_sem, device_id=device, device_id_type=MESH
        )

    def z_copy(n, src, zp, rows, way):
        return remote(src, grad.at[zp, rows, mine], z_send.at[n], z_recv.at[n], dev_z[way])

    def piece(zp, rows, col, width):
        return grad.at[zp, rows, pl.ds(pl.multiple_of(core * PART + col, LANES), width)]

    def z_pass(n, zp, rows, col, width, way):
        part = piece(zp, rows, col, width)
        return remote(part, part, z_send.at[n], z_recv.at[n], dev_z[way])

    def s_copy(n, zp, rows, col=0, width=PART):
        part = piece(zp, rows, col, width)
        return remote(part, part, s_send.at[n], s_recv.at[n], dev_sib)

    z_own = [
        z_copy(0, g_ref.at[h0], z, h0, 0),
        z_copy(1, g_ref.at[h1], z, h1, 1),
        z_copy(2, g_ref.at[h1], z, h1, 0),
        z_copy(3, g_ref.at[h0], z, h0, 1),
    ]
    s_own = remote(g_ref, grad.at[z, :, mine], s_send.at[0], s_recv.at[0], dev_sib)
    z_own[0].start()
    z_own[1].start()
    s_own.start()
    z_fwd = [
        z_pass(4, z_left, h0, 0, CUT, 0),
        z_pass(5, z_right, h1, 0, CUT, 1),
        z_pass(6, z_left, h0, CUT, PART - CUT, 0),
        z_pass(7, z_right, h1, CUT, PART - CUT, 1),
    ]
    s_fwd = [
        s_copy(1, z_left, h0),
        s_copy(2, z_right, h1),
        s_copy(3, z_left, h1),
        s_copy(4, z_right, h0),
        s_copy(5, z_far, h0, 0, CUT),
        s_copy(6, z_far, h1, 0, CUT),
        s_copy(7, z_far, h0, CUT, PART - CUT),
        s_copy(8, z_far, h1, CUT, PART - CUT),
    ]

    wg[pl.ds(NBLK, GROUP), :] = jnp.zeros((GROUP, LANES), jnp.float32)

    u_copy.wait()
    for load in loads[:3]:
        load.start()

    def gelu(n, carry):
        tok = pl.ds(pl.multiple_of(lax.rem(n, 4) * LANES, LANES), LANES)
        hid = pl.ds(pl.multiple_of((n // 4) * LANES, LANES), LANES)
        values = u_buf[tok, hid].astype(jnp.float32)
        cdf = 0.5 * (1.0 + lax.erf(values * half_root))
        density = jnp.exp(-0.5 * values * values) * inv_root_tau
        act_t[hid, tok] = (values * cdf).T.astype(jnp.bfloat16)
        slope[tok, hid] = cdf + values * density
        return carry

    lax.fori_loop(0, 4 * (HID // LANES), gelu, 0)

    def weight_grad(zp, n, part_cols, width):
        cols = pl.ds(pl.multiple_of(part_cols + n * width, LANES), width)
        first = zp * (PAIR // LANES) + (part_cols + n * width) // LANES
        for half in range(2):
            product = jnp.dot(
                act_t[pl.ds(half * PART, PART), :], grad[zp, :, cols], preferred_element_type=jnp.float32
            )
            for c in range(width // LANES):
                row = pl.multiple_of((first + c) * HID + half * PART, LANES)
                wg[pl.ds(row, PART), :] = product[:, c * LANES : (c + 1) * LANES]

    def weight_grad_pair(zp):
        def body(n, carry):
            weight_grad(zp, n, 0, 256)
            return carry

        lax.fori_loop(0, PAIR // 256, body, 0)

    def pre_product(zp, slot, rows, mode, low=0, high=HID // 256):
        def body(n, carry):
            hid = pl.ds(pl.multiple_of(n * 256, LANES), 256)
            product = lax.dot_general(
                grad[zp, rows, :], wbuf[slot, hid, :], (((1,), (1,)), ((), ())),
                preferred_element_type=jnp.float32,
            )
            if mode == "first":
                acc[rows, hid] = product
            elif mode == "add":
                acc[rows, hid] += product
            else:
                pre_ref[rows, hid] = ((acc[rows, hid] + product) * slope[rows, hid]).astype(jnp.bfloat16)
            return carry

        lax.fori_loop(low, high, body, 0)

    whole = pl.ds(0, TOK)
    own_copy.wait()
    s_own.wait_recv()
    weight_grad_pair(z)
    z_own[2].start()
    z_own[3].start()
    loads[0].wait()
    pre_product(z, 0, whole, "first")
    loads[3].start()
    z_own[0].wait_recv()
    s_fwd[0].start()
    z_own[1].wait_recv()
    s_fwd[1].start()
    loads[1].wait()
    loads[2].wait()
    s_fwd[0].wait_recv()
    pre_product(z_left, 1, h0, "add")
    s_fwd[1].wait_recv()
    pre_product(z_right, 2, h1, "add")
    z_fwd[0].start()
    z_fwd[1].start()
    z_own[2].wait_recv()
    s_fwd[2].start()
    z_own[3].wait_recv()
    s_fwd[3].start()
    z_fwd[2].start()
    z_fwd[3].start()
    s_fwd[2].wait_recv()
    weight_grad_pair(z_left)
    z_fwd[0].wait_recv()
    s_fwd[4].start()
    z_fwd[1].wait_recv()
    s_fwd[5].start()
    s_fwd[3].wait_recv()
    weight_grad_pair(z_right)
    weight_grad(z_far, 0, core * PART, CUT)
    for way in range(2):
        s_fwd[4 + way].wait_recv()
    weight_grad(z_far, 0, (1 - core) * PART, CUT)
    for way in range(2):
        z_fwd[2 + way].wait_recv()
        s_fwd[6 + way].start()
    weight_grad(z_far, 0, core * PART + CUT, PART - CUT)
    for way in range(2):
        s_fwd[6 + way].wait_recv()
    weight_grad(z_far, 0, (1 - core) * PART + CUT, PART - CUT)

    scale = 1.0 / math.sqrt(TOK * 16)
    FAR, NEXT, PREV, OWN = range(4)
    SHIFT = (2, 1, -1, 0)
    parts = ((FAR,), (NEXT, PREV), (OWN,))
    send = (send_a, send_b)
    bufs = (
        ((f1a, l1a, r1a), (f2a, l2a, r2a)),
        ((f1b, l1b, r1b), (f2b, l2b, r2b)),
    )

    def axis(half, level):
        along_x = half == level
        places = tuple(step(x if along_x else y, shift) for shift in SHIFT)
        devices = tuple((y * 4 + p, mp) if along_x else (p * 4 + x, mp) for p in places)
        return places, devices

    def gather(half, part, place, row, count):
        low = SPLIT[half][0]
        one = axis(half, 0)[0][place]
        regions = []
        for second in parts[part]:
            two = axis(half, 1)[0][second]
            regions.append((second, (two * 4 + one if half == 0 else one * 4 + two) * SLOTS + low))

        def body(n, carry):
            at = pl.multiple_of(row + n * GROUP, GROUP)
            for second, first in regions:
                taken = [wg[pl.ds(src_ref[0, first + at + s], 1), :] for s in range(GROUP)]
                send[half][second, place, pl.ds(at, GROUP), :] = (
                    jnp.concatenate(taken, axis=0) * scale
                ).astype(jnp.bfloat16)
            return carry

        lax.fori_loop(0, count // GROUP, body, 0)

    def scatter_first(half, part):
        devices = axis(half, 0)[1]
        lead = pl.ds(parts[part][0], len(parts[part]))
        base = 32 * half + 3 * part

        def copy(place, dst):
            return remote(
                send[half].at[lead, place], dst.at[lead], d_send.at[base + place], d_recv.at[base + place],
                devices[place],
            )

        far, left, right = bufs[half][0]
        return (copy(FAR, far), copy(NEXT, left), copy(PREV, right))

    def scatter_second(half):
        devices = axis(half, 1)[1]
        far, left, right = bufs[half][1]

        def copy(n, place, dst):
            return remote(
                send[half].at[place, OWN], dst,
                d_send.at[32 * half + 12 + n], d_recv.at[32 * half + 12 + n], devices[place],
            )

        return (copy(0, FAR, far), copy(1, NEXT, left), copy(2, PREV, right))

    def add_first(half, part):
        far, left, right = bufs[half][0]
        for second in parts[part]:
            send[half][second, OWN] = (
                send[half][second, OWN].astype(jnp.float32)
                + far[second].astype(jnp.float32)
                + left[second].astype(jnp.float32)
                + right[second].astype(jnp.float32)
            ).astype(jnp.bfloat16)

    def add_second(half):
        low, a, b = SPLIT[half]
        far, left, right = bufs[half][1]
        out_ref[y, x, pl.ds(low, a + b), :] = (
            send[half][OWN, OWN].astype(jnp.float32)
            + far[...].astype(jnp.float32)
            + left[...].astype(jnp.float32)
            + right[...].astype(jnp.float32)
        ).astype(jnp.bfloat16)

    first = [[scatter_first(half, part) for part in range(3)] for half in range(2)]
    second = [scatter_second(half) for half in range(2)]

    for part in range(3):
        for place in (FAR, NEXT, PREV):
            for half in range(2):
                gather(half, part, place, 0, SPLIT[half][1] + SPLIT[half][2])
                first[half][part][place].start()
    for part in range(3):
        for half in range(2):
            gather(half, part, OWN, 0, SPLIT[half][1] + SPLIT[half][2])
    for part in range(3):
        for half in range(2):
            for copy in first[half][part]:
                copy.wait_recv()
            add_first(half, part)
            for place in parts[part]:
                if place != OWN:
                    second[half][place].start()
        if part == 0:
            pre_product(z_left, 1, h1, "add")
        elif part == 1:
            pre_product(z_right, 2, h0, "add")

    def spread_copies(half):
        low, a, b = SPLIT[half]
        devices = axis(half, 1)[1]
        part = out_ref.at[y, x, pl.ds(low, a + b)]
        base = 32 * half + 15
        return [
            remote(part, part, d_send.at[base + place], d_recv.at[base + place], devices[place])
            for place in (FAR, NEXT, PREV)
        ]

    def region_copies(half, place):
        low, a, b = SPLIT[half]
        places, devices = axis(half, 0)
        q = axis(half, 1)[0][place]
        base = 32 * half + 18 + 3 * place

        def copy(n, column, row, count, way):
            rows = pl.ds(low + row, count)
            part = out_ref.at[q, column, rows] if half == 0 else out_ref.at[column, q, rows]
            return remote(part, part, d_send.at[base + n], d_recv.at[base + n], devices[way])

        return tuple(copy(n, places[OWN], 0, a + b, way) for n, way in enumerate((NEXT, PREV, FAR)))

    third = [spread_copies(half) for half in range(2)]
    fourth = [[region_copies(half, place) for place in range(4)] for half in range(2)]

    def send_region(half, place):
        for copy in fourth[half][place]:
            copy.start()

    for half in range(2):
        for copy in second[half]:
            copy.wait_recv()
        add_second(half)
        for place in (NEXT, PREV, FAR):
            third[half][place].start()
    for half in range(2):
        send_region(half, OWN)
    loads[3].wait()
    pre_product(z_far, 0, whole, "last", 0, 3)
    for place, arrived in ((NEXT, PREV), (PREV, NEXT), (FAR, FAR)):
        for half in range(2):
            third[half][arrived].wait_recv()
            send_region(half, place)
    pre_product(z_far, 0, whole, "last", 3)
    pre_copy = pltpu.make_async_copy(pre_ref, pre_out, local_sem.at[2])
    pre_copy.start()
    stores = []
    for place in (OWN, NEXT, PREV, FAR):
        for half in range(2):
            low, a, b = SPLIT[half]
            for copy in fourth[half][place]:
                copy.wait_recv()
            q, rows = axis(half, 1)[0][place], pl.ds(low, a + b)
            at = (q, slice(None), rows) if half == 0 else (slice(None), q, rows)
            stores.append(pltpu.make_async_copy(out_ref.at[at], sums_out.at[at], out_sem.at[4 * half + place]))
            stores[-1].start()
    for store in stores:
        store.wait()
    pre_copy.wait()

    for copy in (*z_own, s_own, *z_fwd, *s_fwd):
        copy.wait_send()
    for half in range(2):
        groups = (*first[half], second[half], third[half], *fourth[half])
        for copy in (c for group in groups for c in group):
            copy.wait_send()


def fused(u, grad_part, weights, source):
    rows_a = SPLIT[0][1] + SPLIT[0][2]
    rows_b = SPLIT[1][1] + SPLIT[1][2]
    big = [pltpu.VMEM((4, rows, LANES), jnp.bfloat16) for rows in (rows_a, rows_b) for _ in range(3)]
    small = [pltpu.VMEM((rows, LANES), jnp.bfloat16) for rows in (rows_a, rows_b) for _ in range(3)]
    vmem = pl.BlockSpec(memory_space=pltpu.VMEM)
    hbm = pl.BlockSpec(memory_space=pl.ANY)
    return pl.pallas_call(
        kernel,
        out_shape=(
            jax.ShapeDtypeStruct((TOK, HID), jnp.bfloat16),
            jax.ShapeDtypeStruct((4, 4, KEEP, LANES), jnp.bfloat16),
        ),
        in_specs=[hbm, hbm, hbm, pl.BlockSpec(memory_space=pltpu.SMEM)],
        out_specs=(hbm, hbm),
        scratch_shapes=[
            pltpu.VMEM((NBLK + GROUP, LANES), jnp.float32),
            pltpu.VMEM((3, HID, PAIR), jnp.bfloat16),
            pltpu.VMEM((4, TOK, PAIR), jnp.bfloat16),
            pltpu.VMEM((HID, TOK), jnp.bfloat16),
            pltpu.VMEM((TOK, HID), jnp.float32),
            pltpu.VMEM((TOK, HID), jnp.float32),
            pltpu.VMEM((4, 4, rows_a, LANES), jnp.bfloat16),
            pltpu.VMEM((4, 4, rows_b, LANES), jnp.bfloat16),
            pltpu.VMEM((4, 4, KEEP, LANES), jnp.bfloat16),
            pltpu.VMEM((TOK, HID), jnp.bfloat16),
            pltpu.VMEM((TOK, HID), jnp.bfloat16),
            *big,
            *small,
            pltpu.SemaphoreType.DMA((3,)),
            pltpu.SemaphoreType.DMA((8,)),
            pltpu.SemaphoreType.DMA((4,)),
            pltpu.SemaphoreType.DMA((8,)),
            pltpu.SemaphoreType.DMA((8,)),
            pltpu.SemaphoreType.DMA((9,)),
            pltpu.SemaphoreType.DMA((9,)),
            pltpu.SemaphoreType.DMA((64,)),
            pltpu.SemaphoreType.DMA((64,)),
        ],
        compiler_params=pltpu.CompilerParams(
            collective_id=0, has_side_effects=True, vmem_limit_bytes=57 * 1024 * 1024
        ),
        cost_estimate=pl.CostEstimate(
            flops=4 * TOK * HID * WIDTH, bytes_accessed=20_000_000, transcendentals=2 * TOK * HID
        ),
    )(u, grad_part, weights, source)


FINISH = 4


def finish_kernel(pre_ref, sums_ref, pre_out, sums_out, pre_buf, sums_buf, wide_buf, in_sem, out_sem):
    slots = 16 * KEEP // FINISH
    pre_in = pltpu.make_async_copy(pre_ref, pre_buf, in_sem.at[FINISH])
    pre_back = pltpu.make_async_copy(pre_buf, pre_out, out_sem.at[FINISH])
    parts = [pl.ds(n * slots, slots) for n in range(FINISH)]
    loads = [pltpu.make_async_copy(sums_ref.at[part], sums_buf.at[part], in_sem.at[n]) for n, part in enumerate(parts)]
    stores = [pltpu.make_async_copy(wide_buf.at[part], sums_out.at[part], out_sem.at[n]) for n, part in enumerate(parts)]
    for load in loads:
        load.start()
    pre_in.start()
    for part, load, store in zip(parts, loads, stores):
        load.wait()
        wide_buf[part, :] = sums_buf[part, :].astype(jnp.float32)
        store.start()
    pre_in.wait()
    pre_back.start()
    for store in stores:
        store.wait()
    pre_back.wait()


def finish(pre_grad, sums):
    hbm = pl.BlockSpec(memory_space=pltpu.HBM)
    return pl.pallas_call(
        finish_kernel,
        out_shape=(
            jax.ShapeDtypeStruct((TOK, HID), jnp.bfloat16),
            jax.ShapeDtypeStruct((16 * KEEP, LANES), jnp.float32),
        ),
        in_specs=[hbm, hbm],
        out_specs=(hbm, hbm),
        scratch_shapes=[
            pltpu.VMEM((TOK, HID), jnp.bfloat16),
            pltpu.VMEM((16 * KEEP, LANES), jnp.bfloat16),
            pltpu.VMEM((16 * KEEP, LANES), jnp.float32),
            pltpu.SemaphoreType.DMA((FINISH + 1,)),
            pltpu.SemaphoreType.DMA((FINISH + 1,)),
        ],
    )(pre_grad, sums)


def local(
    inner_before_nonlinear,
    layer_exit_derivative,
    contract_weights,
    copy_tile_indicator,
    span_opening_tile,
    remaining_tile_flags,
):
    source = slot_sources(
        remaining_tile_flags.reshape(ROWS, LANES), copy_tile_indicator.reshape(ROWS, LANES), span_opening_tile
    )
    pre_grad, sums = fused(inner_before_nonlinear, layer_exit_derivative, contract_weights, source)
    pre_grad, sums = finish(pre_grad, sums.reshape(16 * KEEP, LANES))
    return (pre_grad, sums[None])


def solution(mesh):
    in_specs = (
        P("dp", "mp"),
        P("dp", "mp"),
        P("mp", None),
        P("dp", "mp", None),
        P(),
        P("mp", None),
    )
    out_specs = (P("dp", "mp"), P("mp", None, None))
    return jax.shard_map(local, mesh=mesh, in_specs=in_specs, out_specs=out_specs, check_vma=False)
```
